256 devices in a mesh: dp: 32 (over y, x, core), section: 8 (over z).
Axes of the slice: x: 4, y: 4, z: 8, core: 2. Of those that a mesh axis runs over, the one named last changes fastest.
Arguments:
- prompts: bfloat16 [9216, 5120], P('dp'), may hold values from -6 to 6
- dest_replica: int32 [32, 32], P('dp'), may hold values from 0 to 31, as said below
- anchor_start: int32 [32, 32], P('dp'), may hold values from 0 to 279, as said below
- pack_anchor: int32 [32, 32], P('dp'), may hold values from 0 to 31, as said below
- prompt_lengths: int32 [32, 32], P('dp'), may hold values from 7 to 9, as said below
- item_pos: int32 [32, 32, 6], P('dp'), may hold values from 0 to 8, as said below
- logged_order: int32 [32, 32, 6], P('dp'), may hold values from 0 to 5, each once within a row
- norm_gain: float32 [8, 5120], P('section'), may hold values from 0.1 to 1.9
- query_map: bfloat16 [8, 128, 128], P('section'), may hold values from -0.5 to 0.5
- key_map: bfloat16 [8, 5120, 512], P('section'), may hold values from -0.078125 to 0.078125
- value_map: bfloat16 [8, 5120, 512], P('section'), may hold values from -0.078125 to 0.078125
- final_gain: float32 [5120], replicated, may hold values from 0.1 to 1.9
- score_vector: bfloat16 [5120], replicated, may hold values from -0.078125 to 0.078125
Outputs:
- slate_loglik: float32 [1024], P(('dp', 'section'))
The draws below stay inside these ranges and needn't reach their ends.
Inputs may be any that keep to these rules, and one draw needn't show every extreme that they name: `dest_replica`: each row lists every replica once: the destinations of the replica's held prompts in row order. `anchor_start`: a replica's held prompts lie back to back from row 0 in the order of their index, each as long as prompt_lengths gives it at its destination. `pack_anchor`: each row lists every replica once. `prompt_lengths`: the 8 prompts of each micro-batch hold exactly 64 tokens together. `item_pos`: distinct and increasing, below the prompt's length; the last is the prompt's final token. `logged_order`: each row is a permutation of 0 to 5.
All inputs are finite; a program needn't handle non-finite values.
Results may differ from the reference program's by a relative error of at most 0.0085.
Values may be sent and summed in bfloat16 or wider, within the bound.
A program may use at most 128 MiB of HBM per device.

```python
import jax
import jax.numpy as jnp
from jax import lax

D = 5120
HEAD_DIM = 128
KV_HEADS = 4
LMAX = 9
LMIN = 7
ITEMS = 6
MICRO = 4
PER_MB = 8
ROWS_MB = 64
ROWS_O = 288
N_DP = 32
N_SECTION = 8


def plan_layout(key):
    keys_all = jax.random.split(key, 5)
    half_count = PER_MB // 2
    paired = jax.random.randint(keys_all[0], (N_DP, MICRO, half_count), LMIN, LMAX + 1)
    longest = jax.random.randint(keys_all[1], (), 0, N_DP * MICRO * half_count)
    flat_ids = jnp.arange(N_DP * MICRO * half_count).reshape(N_DP, MICRO, half_count)
    paired = jnp.where(flat_ids == longest, LMAX, paired)
    lengths_mb = jnp.concatenate([paired, LMIN + LMAX - paired], axis=2)
    shuffle = jnp.argsort(jax.random.randint(keys_all[2], (N_DP, MICRO, PER_MB), 0, 2 ** 20) * PER_MB + jnp.arange(PER_MB), axis=2)
    lengths_mb = jnp.take_along_axis(lengths_mb, shuffle, axis=2).reshape(N_DP, N_DP)
    senders = jnp.argsort(jax.random.randint(keys_all[3], (N_DP, N_DP), 0, 2 ** 20) * N_DP + jnp.arange(N_DP), axis=1)
    slot_of = jnp.argsort(senders, axis=1)
    from_anchor = jnp.take_along_axis(lengths_mb, slot_of, axis=1).T
    targets = jnp.argsort(jax.random.randint(keys_all[4], (N_DP, N_DP), 0, 2 ** 20) * N_DP + jnp.arange(N_DP), axis=1)
    anchor_lengths = jnp.take_along_axis(from_anchor, targets, axis=1)
    starts = jnp.cumsum(anchor_lengths, axis=1) - anchor_lengths
    return (lengths_mb.astype(jnp.int32), senders.astype(jnp.int32), targets.astype(jnp.int32), starts.astype(jnp.int32))


def draw_dest_replica(key, part):
    shared = plan_layout(key)
    return shared[2]


def draw_anchor_start(key, part):
    shared = plan_layout(key)
    return shared[3]


def draw_pack_anchor(key, part):
    shared = plan_layout(key)
    return shared[1]


def draw_prompt_lengths(key, part):
    shared = plan_layout(key)
    return shared[0]


def draw_item_pos(key, part):
    shared = plan_layout(key)
    key = jax.random.fold_in(key, 15)
    lengths_mb = shared[0]
    spots = jnp.arange(LMAX)
    ranks = jax.random.randint(key, (N_DP, N_DP, LMAX), 0, 2 ** 16) * LMAX + spots
    ranks = jnp.where(spots[None, None, :] == lengths_mb[:, :, None] - 1, 2 ** 16 * LMAX + LMAX, ranks)
    ranks = jnp.where(spots[None, None, :] < lengths_mb[:, :, None], ranks, -1)
    picked = lax.top_k(ranks, ITEMS)[1]
    return jnp.sort(picked, axis=-1).astype(jnp.int32)


def block_levels(key, extent, cuts, least, largest):
    gain, own = 1.0, jax.random.fold_in(key, 6)
    for dim, blocks in cuts:
        draws = jnp.exp(jax.random.uniform(jax.random.fold_in(own, dim), (blocks,), jnp.float32, least / len(cuts), largest / len(cuts)))
        gain = gain * jnp.repeat(draws, extent[dim] // blocks).reshape([-1 if axis == dim else 1 for axis in range(len(extent))])
    return gain


def gaussian(stream_key, extent, deviation, reach, pieces=(), kind=jnp.bfloat16):
    entries = deviation * jax.random.normal(stream_key, extent, jnp.float32)
    if pieces:
        entries = entries * block_levels(stream_key, extent, pieces, -0.22, 0.18)
    return jnp.clip(entries, -reach, reach).astype(kind)


def setup_inputs(seed: int = 0) -> dict:
    seeds = jax.random.split(jax.random.key(seed), 14)
    return {
        "prompts": gaussian(seeds[0], (N_DP * ROWS_O, D), 1.0, 6.0, ((0, 32),)),
        "dest_replica": draw_dest_replica(jax.random.fold_in(seeds[13], 71), 0),
        "anchor_start": draw_anchor_start(jax.random.fold_in(seeds[13], 71), 0),
        "pack_anchor": draw_pack_anchor(jax.random.fold_in(seeds[13], 71), 0),
        "prompt_lengths": draw_prompt_lengths(jax.random.fold_in(seeds[13], 71), 0),
        "item_pos": draw_item_pos(jax.random.fold_in(seeds[13], 71), 0),
        "logged_order": jax.vmap(lambda own: jax.random.permutation(own, ITEMS))(jax.random.split(seeds[6], N_DP * N_DP)).reshape((N_DP, N_DP, ITEMS)).astype(jnp.int32),
        "norm_gain": jnp.clip(1.0 + 0.18 * jax.random.normal(seeds[7], (N_SECTION, D), jnp.float32), 0.1, 1.9),
        "query_map": gaussian(seeds[8], (N_SECTION, HEAD_DIM, HEAD_DIM), HEAD_DIM ** -0.5, 0.5, ((0, 8),)),
        "key_map": gaussian(seeds[9], (N_SECTION, D, KV_HEADS * HEAD_DIM), D ** -0.5, 0.078125, ((0, 8),)),
        "value_map": gaussian(seeds[10], (N_SECTION, D, KV_HEADS * HEAD_DIM), D ** -0.5, 0.078125, ((0, 8),)),
        "final_gain": jnp.clip(1.0 + 0.18 * jax.random.normal(seeds[11], (D,), jnp.float32), 0.1, 1.9),
        "score_vector": gaussian(seeds[12], (D,), D ** -0.5, 0.078125),
    }


epsilon = 1e-06

def rms_scale(vectors, scale_gain):
    return vectors * lax.rsqrt(lax.optimization_barrier(jnp.mean(vectors * vectors, axis=-1, keepdims=True)) + epsilon) * scale_gain

def round_trip(vectors):
    return lax.optimization_barrier(vectors.astype(jnp.bfloat16)).astype(jnp.float32)

def attend_block(tokens, allowed, scale_gain, query_weight, key_weight, value_weight):
    row_count = tokens.shape[0]
    head_width = query_weight.shape[0]
    kv_count = key_weight.shape[1] // head_width
    widths = tokens.astype(jnp.float32)
    normed = rms_scale(widths, scale_gain).astype(jnp.bfloat16)
    heads_in = normed.astype(jnp.float32).reshape(row_count, -1, head_width)
    head_count = heads_in.shape[1]
    group_size = head_count // kv_count
    queries = jnp.einsum('rhd,de->rhe', heads_in, query_weight.astype(jnp.float32), precision=lax.Precision.HIGHEST)
    queries = round_trip(rms_scale(queries, 1.0)).reshape(row_count, kv_count, group_size, head_width)
    key_heads = jnp.dot(normed, key_weight, preferred_element_type=jnp.float32).reshape(row_count, kv_count, head_width)
    key_heads = round_trip(rms_scale(key_heads, 1.0))
    value_heads = round_trip(jnp.dot(normed, value_weight, preferred_element_type=jnp.float32)).reshape(row_count, kv_count, head_width)
    scores = jnp.einsum('rkge,ske->kgrs', queries, key_heads, precision=lax.Precision.HIGHEST) * head_width ** (-0.5)
    raw_weights = jnp.where(allowed[None, None], jnp.exp(scores), 0.0)
    weights = round_trip(raw_weights / lax.optimization_barrier(jnp.sum(raw_weights, axis=-1, keepdims=True)))
    mixture = jnp.einsum('kgrs,skd->rkgd', weights, value_heads, precision=lax.Precision.HIGHEST)
    return (widths + mixture.reshape(row_count, -1)).astype(jnp.bfloat16)

def slate_terms(hidden, item_rows, ranking, final_gain, score_vector):
    picked = hidden[item_rows.reshape(-1)].astype(jnp.float32)
    normed = lax.optimization_barrier(rms_scale(picked, final_gain).astype(jnp.bfloat16))
    scores = jnp.dot(normed, score_vector, preferred_element_type=jnp.float32).reshape(ranking.shape)
    ordered = jnp.take_along_axis(scores, ranking, axis=1)
    tail_sums = jnp.log(jnp.cumsum(jnp.exp(ordered)[:, ::-1], axis=1)[:, ::-1])
    return lax.optimization_barrier(jnp.sum(ordered - tail_sums, axis=1))

def reference(prompts, dest_replica, anchor_start, pack_anchor, prompt_lengths, item_pos, logged_order, norm_gain, query_map, key_map, value_map, final_gain, score_vector):
    replica_ids = jnp.arange(N_DP, dtype=jnp.int32)
    matches = dest_replica[:, :, None] == replica_ids[None, None, :]
    start_for = lax.optimization_barrier(jnp.sum(jnp.where(matches, anchor_start[:, :, None], 0), axis=1)).astype(jnp.int32)
    lengths_all = prompt_lengths.reshape(N_DP * MICRO, PER_MB)
    senders_all = pack_anchor.reshape(N_DP * MICRO, PER_MB)
    items_all = item_pos.reshape(N_DP * MICRO, PER_MB, ITEMS)
    rankings_all = logged_order.reshape(N_DP * MICRO, PER_MB, ITEMS)
    target_all = jnp.repeat(replica_ids, MICRO)
    positions = jnp.arange(ROWS_MB, dtype=jnp.int32)

    def one_batch(inputs):
        lengths_mb, senders, item_ids, ranking, target_replica = inputs
        offsets = (jnp.cumsum(lengths_mb) - lengths_mb).astype(jnp.int32)
        segment = (lax.optimization_barrier(jnp.sum((offsets[None, :] <= positions[:, None]).astype(jnp.int32), axis=1)) - 1).astype(jnp.int32)
        within = (positions - offsets[segment]).astype(jnp.int32)
        starts = start_for[senders, target_replica].astype(jnp.int32)
        source = (senders[segment] * ROWS_O + starts[segment] + within).astype(jnp.int32)
        hidden = prompts[source]
        allowed = (segment[:, None] == segment[None, :]) & (positions[None, :] <= positions[:, None])
        for section_index in range(N_SECTION):
            hidden = attend_block(hidden, allowed, norm_gain[section_index], query_map[section_index], key_map[section_index], value_map[section_index])
        item_rows = (offsets[:, None] + item_ids).astype(jnp.int32)
        return slate_terms(hidden, item_rows, ranking, final_gain, score_vector)
    result = lax.map(one_batch, (lengths_all, senders_all, items_all, rankings_all, target_all))
    return result.reshape(N_DP * N_DP)
```

```python
import functools

import jax
import jax.numpy as jnp
from jax import lax
from jax.experimental import pallas as pl
from jax.experimental.pallas import tpu as pltpu
from jax.sharding import PartitionSpec as P

EPS = 1e-06
HEAD = 128
GROUPS = 4
ITEMS = 6
LMAX = 9
CHUNK = 16
TAIL = 16
WINDOW = CHUNK + TAIL
PIECES = 4

BF16 = jnp.bfloat16
F32 = jnp.float32
MESH = pl.DeviceIdType.MESH


def iota(shape, dim):
    return lax.broadcasted_iota(jnp.int32, shape, dim)


def kernel(
    sections,
    replicas,
    prompts,
    dest,
    start,
    pack,
    items,
    order,
    gain,
    query,
    key_map,
    value_map,
    final_gain,
    score_vector,
    out,
    x,
    kw,
    vw,
    kv,
    pair,
    kblock,
    vblock,
    bias,
    ones_q,
    ones_k,
    weigh,
    start_row,
    target,
    windows,
    gathered,
    final,
    x_sem,
    w_sem,
    recv_sem,
    send_sem,
    score_send,
    score_recv,
    out_send,
    out_recv,
):
    d = lax.axis_index("dp")
    s = lax.axis_index("section")
    rows_all, width = x.shape
    chunks = rows_all // CHUNK
    last = sections - 1
    heads = width // HEAD
    per_group = heads // GROUPS
    kv_width = GROUPS * HEAD
    above = lax.rem(s + 1, sections)
    below = lax.rem(s + sections - 1, sections)

    def chunk_rows(c):
        return pl.ds(pl.multiple_of(c * CHUNK, 16), CHUNK)

    def x_copy(c):
        return pltpu.make_async_copy(prompts.at[chunk_rows(c)], x.at[chunk_rows(c)], x_sem.at[c])

    def hop(c):
        return pltpu.make_async_remote_copy(
            x.at[chunk_rows(c)], x.at[chunk_rows(c)], send_sem.at[c], recv_sem.at[c],
            device_id=(d, above), device_id_type=MESH,
        )

    piece = width // PIECES

    def w_copies():
        copies = []
        for p in range(PIECES):
            part = pl.ds(p * piece, piece)
            copies.append(pltpu.make_async_copy(key_map.at[0, part], kw.at[part], w_sem.at[0, p]))
            copies.append(pltpu.make_async_copy(value_map.at[0, part], vw.at[part], w_sem.at[1, p]))
        return copies

    @pl.when(s == 0)
    def _():
        x_copy(0).start()

    for copy in w_copies():
        copy.start()

    @pl.when(s == 0)
    def _():
        def fetch(c, carry):
            x_copy(c).start()
            return carry

        lax.fori_loop(1, chunks, fetch, 0)

    barrier = pltpu.get_barrier_semaphore()
    pl.semaphore_signal(barrier, inc=1, device_id=(d, above), device_id_type=MESH)
    pl.semaphore_signal(barrier, inc=1, device_id=(d, below), device_id_type=MESH)

    @pl.when(s < last)
    def _():
        pl.semaphore_signal(barrier, inc=1, device_id=(d, last), device_id_type=MESH)

    @pl.when(s == last)
    def _():
        def greet_section(i, carry):
            pl.semaphore_signal(barrier, inc=1, device_id=(d, i), device_id_type=MESH)
            return carry

        def greet_replica(i, carry):
            peer = lax.rem(d + i, replicas)
            pl.semaphore_signal(barrier, inc=1, device_id=(peer, last), device_id_type=MESH)
            return carry

        lax.fori_loop(0, last, greet_section, 0)
        lax.fori_loop(1, replicas, greet_replica, 0)

    pair[...] = jnp.zeros_like(pair)
    pair[0:HEAD, 0:HEAD] = query[0]
    pair[HEAD : 2 * HEAD, HEAD : 2 * HEAD] = query[0]
    kblock[...] = jnp.zeros_like(kblock)
    vblock[...] = jnp.zeros_like(vblock)
    kv[0:TAIL, :] = jnp.zeros((TAIL, 2 * kv_width), BF16)
    ones_q[...] = jnp.where(
        iota(ones_q.shape, 0) // HEAD == iota(ones_q.shape, 1) // WINDOW, 1.0, 0.0
    ).astype(BF16)
    ones_k[...] = jnp.where(
        iota(ones_k.shape, 0) // WINDOW == iota(ones_k.shape, 1) // WINDOW, 1.0, 0.0
    ).astype(BF16)

    starts = start[...].astype(F32)
    for c in range(chunks):
        row = (iota((CHUNK, replicas), 0) + c * CHUNK).astype(F32)
        first = jnp.max(jnp.where(starts <= row, starts, 0.0), axis=1, keepdims=True)
        seen = (iota((CHUNK, GROUPS * WINDOW), 1) % WINDOW + c * CHUNK - TAIL).astype(F32)
        own = (iota((CHUNK, GROUPS * WINDOW), 0) + c * CHUNK).astype(F32)
        bias[c] = jnp.where((seen >= first) & (seen <= own), 0.0, -1e30)

    square = (replicas, replicas)

    @pl.when(s == last)
    def _():
        weigh[...] = final_gain[...] * score_vector[...].astype(F32).reshape(1, width)
        column = jnp.sum(
            jnp.where(dest[...] == iota(square, 0), starts, 0.0), axis=1, keepdims=True
        )
        start_row[0:1, 0:replicas] = jnp.sum(
            jnp.where(iota(square, 0) == iota(square, 1), column, 0.0), axis=0, keepdims=True
        )
        origin = pack[...].astype(F32) * 16.0
        for k in range(ITEMS):
            place = origin
            for i in range(ITEMS):
                place = place + jnp.where(order[k] == i, items[i].astype(F32), 0.0)
            target[k : k + 1, 0:replicas] = place
        windows[...] = jnp.zeros_like(windows)

    @pl.when(s < last)
    def _():
        pl.semaphore_wait(barrier, 3)

    @pl.when(s == last)
    def _():
        pl.semaphore_wait(barrier, last + replicas + 1)

    for copy in w_copies():
        copy.wait()

    def scale_of(states):
        return lax.rsqrt(jnp.mean(states * states, axis=1, keepdims=True) + EPS)

    def by_group(values):
        def head(a):
            p, half = divmod(a, 2)
            return values[p * CHUNK : (p + 1) * CHUNK, half * HEAD : (half + 1) * HEAD]

        return jnp.concatenate(
            [
                jnp.concatenate([head(b * per_group + j) for b in range(GROUPS)], axis=1)
                for j in range(per_group)
            ],
            axis=0,
        )

    def block(c):
        states = x[chunk_rows(c), :].astype(F32)
        normed = (states * scale_of(states) * gain[...]).astype(BF16)
        keys = jnp.dot(normed, kw[...], preferred_element_type=F32)
        parts = []
        for b in range(GROUPS):
            head = keys[:, b * HEAD : (b + 1) * HEAD]
            parts.append((head * scale_of(head)).astype(BF16))
        parts.append(jnp.dot(normed, vw[...], preferred_element_type=F32).astype(BF16))
        fresh = jnp.concatenate(parts, axis=1)
        old = kv[...]
        kv[...] = fresh
        stacked = jnp.concatenate(
            [normed[:, p * 2 * HEAD : (p + 1) * 2 * HEAD] for p in range(heads // 2)], axis=0
        )
        q = jnp.dot(stacked, pair[...], preferred_element_type=F32)
        squares = jnp.dot(by_group((q * q).astype(BF16)), ones_q[...], preferred_element_type=F32)
        for b in range(GROUPS):
            cols = slice(b * HEAD, (b + 1) * HEAD)
            more = slice(kv_width + b * HEAD, kv_width + (b + 1) * HEAD)
            for place, part in ((0, old), (TAIL, fresh)):
                rows = slice(b * WINDOW + place, b * WINDOW + place + 16)
                kblock[rows, cols] = part[:, cols]
                vblock[rows, cols] = part[:, more]
        raw = lax.dot_general(
            by_group(q.astype(BF16)), kblock[...], (((1,), (1,)), ((), ())), preferred_element_type=F32
        )
        scores = raw * (lax.rsqrt(squares * (1.0 / HEAD) + EPS) * HEAD ** (-0.5))
        powers = jnp.exp(scores + jnp.concatenate([bias[c]] * per_group, axis=0))
        total = jnp.dot(powers.astype(BF16), ones_k[...], preferred_element_type=F32)
        weights = (powers / total).astype(BF16)
        mixed = jnp.dot(weights, vblock[...], preferred_element_type=F32)
        placed = [
            mixed[j * CHUNK : (j + 1) * CHUNK, b * HEAD : (b + 1) * HEAD]
            for b in range(GROUPS)
            for j in range(per_group)
        ]
        x[chunk_rows(c), :] = (states + jnp.concatenate(placed, axis=1)).astype(BF16)

    def finish(c):
        states = x[chunk_rows(c), :].astype(F32)
        value = jnp.sum(states * weigh[...], axis=1, keepdims=True) * scale_of(states)
        row = (iota((CHUNK, replicas), 0) + c * CHUNK).astype(F32)
        offset = row - start_row[0:1, 0:replicas]
        found = [
            jnp.sum(jnp.where(offset == float(i), value, 0.0), axis=0, keepdims=True) for i in range(LMAX)
        ]
        found.append(jnp.zeros((16 - LMAX, replicas), F32))
        windows[:, 0:replicas] += jnp.concatenate(found, axis=0)

    def advance(c, carry):
        @pl.when(s == 0)
        def _():
            x_copy(c).wait()

        @pl.when(s > 0)
        def _():
            hop(c).wait_recv()

        block(c)

        @pl.when(s < last)
        def _():
            hop(c).start()

        @pl.when(s == last)
        def _():
            finish(c)

        return carry

    lax.fori_loop(0, chunks, advance, 0)

    @pl.when(s == last)
    def _():
        def score_copy(peer, slot):
            return pltpu.make_async_remote_copy(
                windows, gathered.at[slot], score_send.at[peer], score_recv.at[slot],
                device_id=(peer, last), device_id_type=MESH,
            )

        def send(i, carry):
            score_copy(lax.rem(d + i, replicas), d).start()
            return carry

        def receive(i, carry):
            peer = lax.rem(d + i, replicas)
            score_copy(peer, peer).wait_recv()
            return carry

        def sent(i, carry):
            score_copy(lax.rem(d + i, replicas), d).wait_send()
            return carry

        lax.fori_loop(1, replicas, send, 0)
        gathered[d] = windows[...]
        lax.fori_loop(1, replicas, receive, 0)
        mine = jnp.sum(
            jnp.where(iota(gathered.shape, 2) == d, gathered[...], 0.0), axis=2, keepdims=True
        ).reshape(replicas * 16, 1)
        place = iota((replicas * 16, replicas), 0).astype(F32)
        ordered = [
            jnp.sum(jnp.where(place == target[k : k + 1, 0:replicas], mine, 0.0), axis=0, keepdims=True)
            for k in range(ITEMS)
        ]
        tail = jnp.zeros((1, replicas), F32)
        total = jnp.zeros((1, replicas), F32)
        for k in reversed(range(ITEMS)):
            tail = tail + jnp.exp(ordered[k])
            total = total + (ordered[k] - jnp.log(tail))
        final[0:1, 0:replicas] = total

        def out_copy(i):
            return pltpu.make_async_remote_copy(
                final, final, out_send.at[i], out_recv.at[0], device_id=(d, i), device_id_type=MESH
            )

        def send_out(i, carry):
            out_copy(i).start()
            return carry

        def sent_out(i, carry):
            out_copy(i).wait_send()
            return carry

        lax.fori_loop(0, last, send_out, 0)
        lax.fori_loop(1, replicas, sent, 0)
        lax.fori_loop(0, last, sent_out, 0)

    @pl.when(s < last)
    def _():
        def sent_hop(c, carry):
            hop(c).wait_send()
            return carry

        lax.fori_loop(0, chunks, sent_hop, 0)

    @pl.when(s < last)
    def _():
        pltpu.make_async_remote_copy(
            final, final, out_send.at[0], out_recv.at[0], device_id=(d, last), device_id_type=MESH
        ).wait_recv()

    values = final[0:1, :]
    share = replicas // sections
    for j in range(share):
        out[j] = jnp.sum(jnp.where(iota(values.shape, 1) == s * share + j, values, 0.0))


def body(
    prompts,
    dest_replica,
    anchor_start,
    pack_anchor,
    prompt_lengths,
    item_pos,
    logged_order,
    norm_gain,
    query_map,
    key_map,
    value_map,
    final_gain,
    score_vector,
):
    sections = lax.axis_size("section")
    replicas = lax.axis_size("dp")
    rows, width = prompts.shape
    chunks = rows // CHUNK
    kv_width = GROUPS * HEAD
    whole = pl.BlockSpec(memory_space=pltpu.VMEM)
    held = pl.BlockSpec(memory_space=pl.ANY)
    return pl.pallas_call(
        functools.partial(kernel, sections, replicas),
        out_shape=jax.ShapeDtypeStruct((replicas // sections,), F32),
        in_specs=[held] + [whole] * 7 + [held, held] + [whole] * 2,
        out_specs=pl.BlockSpec(memory_space=pltpu.SMEM),
        scratch_shapes=[
            pltpu.VMEM((rows, width), BF16),
            pltpu.VMEM((width, kv_width), BF16),
            pltpu.VMEM((width, kv_width), BF16),
            pltpu.VMEM((TAIL, 2 * kv_width), BF16),
            pltpu.VMEM((2 * HEAD, 2 * HEAD), BF16),
            pltpu.VMEM((GROUPS * WINDOW, kv_width), BF16),
            pltpu.VMEM((GROUPS * WINDOW, kv_width), BF16),
            pltpu.VMEM((chunks, CHUNK, GROUPS * WINDOW), F32),
            pltpu.VMEM((kv_width, GROUPS * WINDOW), BF16),
            pltpu.VMEM((GROUPS * WINDOW, GROUPS * WINDOW), BF16),
            pltpu.VMEM((1, width), F32),
            pltpu.VMEM((8, 128), F32),
            pltpu.VMEM((8, 128), F32),
            pltpu.VMEM((16, 128), F32),
            pltpu.VMEM((replicas, 16, 128), F32),
            pltpu.VMEM((8, 128), F32),
            pltpu.SemaphoreType.DMA((chunks,)),
            pltpu.SemaphoreType.DMA((2, PIECES)),
            pltpu.SemaphoreType.DMA((chunks,)),
            pltpu.SemaphoreType.DMA((chunks,)),
            pltpu.SemaphoreType.DMA((replicas,)),
            pltpu.SemaphoreType.DMA((replicas,)),
            pltpu.SemaphoreType.DMA((sections,)),
            pltpu.SemaphoreType.DMA((1,)),
        ],
        compiler_params=pltpu.CompilerParams(
            collective_id=0, has_side_effects=True, vmem_limit_bytes=56 << 20
        ),
        name="slates",
    )(
        prompts,
        dest_replica,
        anchor_start,
        pack_anchor,
        jnp.transpose(item_pos, (2, 0, 1)),
        jnp.transpose(logged_order, (2, 0, 1)),
        norm_gain,
        query_map,
        key_map,
        value_map,
        final_gain.reshape(1, width),
        score_vector,
    )


def solution(mesh):
    return jax.shard_map(
        body,
        mesh=mesh,
        in_specs=(
            P("dp", None),
            P("dp", None),
            P("dp", None),
            P("dp", None),
            P("dp", None),
            P("dp", None, None),
            P("dp", None, None),
            P("section", None),
            P("section", None, None),
            P("section", None, None),
            P("section", None, None),
            P(),
            P(),
        ),
        out_specs=P(("dp", "section")),
        check_vma=False,
    )
```

```python
import functools

import jax
import jax.numpy as jnp
from jax import lax
from jax.experimental import pallas as pl
from jax.experimental.pallas import tpu as pltpu
from jax.sharding import PartitionSpec as P

EPS = 1e-06
HEAD = 128
GROUPS = 4
ITEMS = 6
LMAX = 9
CHUNK = 16
TAIL = 16
WINDOW = CHUNK + TAIL
PIECES = 4
SPILL = 1024.0
PARTS = 4

BF16 = jnp.bfloat16
F32 = jnp.float32
MESH = pl.DeviceIdType.MESH


def iota(shape, dim):
    return lax.broadcasted_iota(jnp.int32, shape, dim)


def kernel(
    sections,
    replicas,
    prompts,
    dest,
    start,
    pack,
    items,
    order,
    gain,
    query,
    key_map,
    value_map,
    final_gain,
    score_vector,
    out,
    x,
    kw,
    vw,
    kv,
    pair,
    kblock,
    vblock,
    bias,
    ones_q,
    ones_k,
    weigh,
    start_row,
    target,
    windows,
    gathered,
    final,
    x_sem,
    w_sem,
    recv_sem,
    send_sem,
    score_send,
    score_recv,
    out_send,
    out_recv,
    turn,
):
    d = lax.axis_index("dp")
    s = lax.axis_index("section")
    rows_all, width = x.shape
    chunks = rows_all // CHUNK
    last = sections - 1
    heads = width // HEAD
    per_group = heads // GROUPS
    kv_width = GROUPS * HEAD
    above = lax.rem(s + 1, sections)
    below = lax.rem(s + sections - 1, sections)
    twin = d + 1 - 2 * lax.rem(d, 2)

    def chunk_rows(c):
        return pl.ds(pl.multiple_of(c * CHUNK, 16), CHUNK)

    def x_copy(c):
        return pltpu.make_async_copy(prompts.at[chunk_rows(c)], x.at[chunk_rows(c)], x_sem.at[c])

    part = width // PARTS
    part_groups = GROUPS // PARTS

    def hop(c, p):
        block = x.at[chunk_rows(c), pl.ds(p * part, part)]
        return pltpu.make_async_remote_copy(
            block, block, send_sem.at[c, p], recv_sem.at[c, p],
            device_id=(d, above), device_id_type=MESH,
        )

    piece = width // PIECES

    def w_copies():
        copies = []
        for p in range(PIECES):
            part = pl.ds(p * piece, piece)
            copies.append(pltpu.make_async_copy(key_map.at[0, part], kw.at[part], w_sem.at[0, p]))
            copies.append(pltpu.make_async_copy(value_map.at[0, part], vw.at[part], w_sem.at[1, p]))
        return copies

    @pl.when(s == 0)
    def _():
        x_copy(0).start()

    for copy in w_copies():
        copy.start()

    @pl.when(s == 0)
    def _():
        def fetch(c, carry):
            x_copy(c).start()
            return carry

        lax.fori_loop(1, chunks, fetch, 0)

    barrier = pltpu.get_barrier_semaphore()
    pl.semaphore_signal(barrier, inc=1, device_id=(d, above), device_id_type=MESH)
    pl.semaphore_signal(barrier, inc=1, device_id=(d, below), device_id_type=MESH)

    @pl.when(s < last)
    def _():
        pl.semaphore_signal(barrier, inc=1, device_id=(d, last), device_id_type=MESH)

    @pl.when(s == 0)
    def _():
        pl.semaphore_signal(barrier, inc=1, device_id=(twin, s), device_id_type=MESH)

    @pl.when(s == last)
    def _():
        def greet_section(i, carry):
            pl.semaphore_signal(barrier, inc=1, device_id=(d, i), device_id_type=MESH)
            return carry

        def greet_replica(i, carry):
            peer = lax.rem(d + i, replicas)
            pl.semaphore_signal(barrier, inc=1, device_id=(peer, last), device_id_type=MESH)
            return carry

        lax.fori_loop(0, last, greet_section, 0)
        lax.fori_loop(1, replicas, greet_replica, 0)

    pair[...] = jnp.zeros_like(pair)
    pair[0:HEAD, 0:HEAD] = query[0]
    pair[HEAD : 2 * HEAD, HEAD : 2 * HEAD] = query[0]
    kblock[...] = jnp.zeros_like(kblock)
    vblock[...] = jnp.zeros_like(vblock)
    kv[0:TAIL, :] = jnp.zeros((TAIL, 2 * kv_width), BF16)
    ones_q[...] = jnp.where(
        iota(ones_q.shape, 0) // HEAD == iota(ones_q.shape, 1) // WINDOW, 1.0, 0.0
    ).astype(BF16)
    ones_k[...] = jnp.where(
        iota(ones_k.shape, 0) // WINDOW == iota(ones_k.shape, 1) // HEAD, 1.0, 0.0
    ).astype(BF16)

    starts = start[...].astype(F32)
    for c in range(chunks):
        row = (iota((CHUNK, replicas), 0) + c * CHUNK).astype(F32)
        first = jnp.max(jnp.where(starts <= row, starts, 0.0), axis=1, keepdims=True)
        seen = (iota((CHUNK, GROUPS * WINDOW), 1) % WINDOW + c * CHUNK - TAIL).astype(F32)
        own = (iota((CHUNK, GROUPS * WINDOW), 0) + c * CHUNK).astype(F32)
        bias[c] = jnp.where((seen >= first) & (seen <= own), 0.0, -1e30)

    square = (replicas, replicas)

    @pl.when(s == last)
    def _():
        weigh[...] = final_gain[...] * score_vector[...].astype(F32).reshape(1, width)
        column = jnp.sum(
            jnp.where(dest[...] == iota(square, 0), starts, 0.0), axis=1, keepdims=True
        )
        start_row[0:1, 0:replicas] = jnp.sum(
            jnp.where(iota(square, 0) == iota(square, 1), column, 0.0), axis=0, keepdims=True
        )
        away = pack[...] - d
        slot = jnp.where(away < 0, away + replicas, away).astype(F32) * 8.0
        for k in range(ITEMS):
            spot = jnp.zeros((1, replicas), F32)
            for i in range(ITEMS):
                spot = spot + jnp.where(order[k] == i, items[i].astype(F32), 0.0)
            target[k : k + 1, 0:replicas] = jnp.where(spot < 8.0, slot + spot, slot + SPILL)
        windows[...] = jnp.zeros_like(windows)

    @pl.when(s == 0)
    def _():
        pl.semaphore_wait(barrier, 4)

    @pl.when((s > 0) & (s < last))
    def _():
        pl.semaphore_wait(barrier, 3)

    @pl.when(s == last)
    def _():
        pl.semaphore_wait(barrier, last + replicas + 1)

    for copy in w_copies():
        copy.wait()

    def scale_of(states):
        return lax.rsqrt(jnp.mean(states * states, axis=1, keepdims=True) + EPS)

    def by_group(parts):
        def head(b, j):
            a = (b % part_groups) * per_group + j
            p, half = divmod(a, 2)
            values = parts[b // part_groups]
            return values[p * CHUNK : (p + 1) * CHUNK, half * HEAD : (half + 1) * HEAD]

        return jnp.concatenate(
            [jnp.concatenate([head(b, j) for b in range(GROUPS)], axis=1) for j in range(per_group)],
            axis=0,
        )

    def block(c):
        rows = chunk_rows(c)
        old = kv[...]
        energy = jnp.zeros((CHUNK, 1), F32)
        keys = jnp.zeros((CHUNK, kv_width), F32)
        values = jnp.zeros((CHUNK, kv_width), F32)
        queries, squares = [], []
        for p in range(PARTS):
            @pl.when(s > 0)
            def _():
                hop(c, p).wait_recv()

            cols = slice(p * part, (p + 1) * part)
            states = x[rows, cols].astype(F32)
            energy = energy + jnp.sum(states * states, axis=1, keepdims=True)
            gained = (states * gain[:, cols]).astype(BF16)
            keys = keys + jnp.dot(gained, kw[cols, :], preferred_element_type=F32)
            values = values + jnp.dot(gained, vw[cols, :], preferred_element_type=F32)
            stacked = jnp.concatenate(
                [gained[:, i * 2 * HEAD : (i + 1) * 2 * HEAD] for i in range(part // (2 * HEAD))], axis=0
            )
            q = jnp.dot(stacked, pair[...], preferred_element_type=F32)
            queries.append(q.astype(BF16))
            squares.append((q * q).astype(BF16))
        scale = lax.rsqrt(energy * (1.0 / width) + EPS)
        keys = keys * scale
        values = (values * scale).astype(BF16)
        for b in range(GROUPS):
            cols = slice(b * HEAD, (b + 1) * HEAD)
            more = slice(kv_width + b * HEAD, kv_width + (b + 1) * HEAD)
            head = keys[:, cols]
            head = (head * scale_of(head)).astype(BF16)
            kblock[b * WINDOW : b * WINDOW + TAIL, cols] = old[:, cols]
            kblock[b * WINDOW + TAIL : (b + 1) * WINDOW, cols] = head
            kv[:, cols] = head
            vblock[b * WINDOW : b * WINDOW + TAIL, cols] = old[:, more]
            vblock[b * WINDOW + TAIL : (b + 1) * WINDOW, cols] = values[:, cols]
            kv[:, more] = values[:, cols]
        length = jnp.dot(by_group(squares), ones_q[...], preferred_element_type=F32)
        scales = jnp.concatenate([scale] * per_group, axis=0)
        factor = scales * lax.rsqrt(length * (scales * scales * (1.0 / HEAD)) + EPS) * HEAD ** (-0.5)
        raw = lax.dot_general(
            by_group(queries), kblock[...], (((1,), (1,)), ((), ())), preferred_element_type=F32
        )
        powers = jnp.exp(raw * factor + jnp.concatenate([bias[c]] * per_group, axis=0)).astype(BF16)
        for p in range(PARTS):
            near = slice(p * part_groups * HEAD, (p + 1) * part_groups * HEAD)
            cols = slice(p * part, (p + 1) * part)
            mixed = jnp.dot(powers, vblock[:, near], preferred_element_type=F32)
            total = jnp.dot(powers, ones_k[:, near], preferred_element_type=F32)
            mixed = mixed / total
            placed = [
                mixed[j * CHUNK : (j + 1) * CHUNK, b * HEAD : (b + 1) * HEAD]
                for b in range(part_groups)
                for j in range(per_group)
            ]
            x[rows, cols] = (x[rows, cols].astype(F32) + jnp.concatenate(placed, axis=1)).astype(BF16)

            if p == 0:
                @pl.when((s == 0) & (c == 0) & (lax.rem(d, 2) == 1))
                def _():
                    pl.semaphore_wait(turn, 1)

            @pl.when(s < last)
            def _():
                hop(c, p).start()

    def finish(c):
        states = x[chunk_rows(c), :].astype(F32)
        value = jnp.sum(states * weigh[...], axis=1, keepdims=True) * scale_of(states)
        row = (iota((CHUNK, replicas), 0) + c * CHUNK).astype(F32)
        offset = row - start_row[0:1, 0:replicas]
        found = [
            jnp.sum(jnp.where(offset == float(i), value, 0.0), axis=0, keepdims=True) for i in range(LMAX)
        ]
        windows[:, 0:replicas] += jnp.concatenate(found[0:8], axis=0)
        windows[0:1, replicas : 2 * replicas] += found[8]

    def advance(c, carry):
        @pl.when(s == 0)
        def _():
            x_copy(c).wait()

        block(c)

        @pl.when((s == 0) & (c == 0) & (lax.rem(d, 2) == 0))
        def _():
            pl.semaphore_signal(turn, inc=1, device_id=(twin, s), device_id_type=MESH)

        @pl.when(s == last)
        def _():
            finish(c)

        return carry

    lax.fori_loop(0, chunks, advance, 0)

    @pl.when(s == last)
    def _():
        def score_copy(i):
            peer = lax.rem(d + replicas - i, replicas)
            return pltpu.make_async_remote_copy(
                windows, gathered.at[i], score_send.at[0], score_recv.at[0],
                device_id=(peer, last), device_id_type=MESH,
            )

        others = gathered.at[pl.ds(1, replicas - 1)]
        for i in range(1, replicas):
            score_copy(i).start()
        gathered[0] = windows[...]
        pltpu.make_async_copy(others, others, score_recv.at[0]).wait()
        held = gathered[...]
        lane = iota(gathered.shape, 2)
        near = jnp.sum(jnp.where(lane == d, held, 0.0), axis=2, keepdims=True).reshape(replicas * 8, 1)
        far = jnp.sum(jnp.where(lane == d + replicas, held, 0.0), axis=2, keepdims=True)
        far = far.reshape(replicas * 8, 1)
        place = iota((replicas * 8, replicas), 0).astype(F32)
        ordered = []
        for k in range(ITEMS):
            wanted = target[k : k + 1, 0:replicas]
            picked = jnp.where(place == wanted, near, 0.0) + jnp.where(place + SPILL == wanted, far, 0.0)
            ordered.append(jnp.sum(picked, axis=0, keepdims=True))
        tail = jnp.zeros((1, replicas), F32)
        total = jnp.zeros((1, replicas), F32)
        for k in reversed(range(ITEMS)):
            tail = tail + jnp.exp(ordered[k])
            total = total + (ordered[k] - jnp.log(tail))
        final[0:1, 0:replicas] = total

        def out_copy(i):
            return pltpu.make_async_remote_copy(
                final, final, out_send.at[i], out_recv.at[0], device_id=(d, i), device_id_type=MESH
            )

        for i in sorted(range(last), key=lambda i: -min(i + 1, last - i)):
            out_copy(i).start()
        pltpu.make_async_copy(others, others, score_send.at[0]).wait()
        for i in range(last):
            out_copy(i).wait_send()

    @pl.when(s < last)
    def _():
        def sent_hop(c, carry):
            for p in range(PARTS):
                hop(c, p).wait_send()
            return carry

        lax.fori_loop(0, chunks, sent_hop, 0)

    @pl.when(s < last)
    def _():
        pltpu.make_async_remote_copy(
            final, final, out_send.at[0], out_recv.at[0], device_id=(d, last), device_id_type=MESH
        ).wait_recv()

    values = final[...]
    share = replicas // sections
    for j in range(share):
        out[j] = jnp.sum(jnp.where(iota(values.shape, 1) == s * share + j, values, 0.0))


def body(
    prompts,
    dest_replica,
    anchor_start,
    pack_anchor,
    prompt_lengths,
    item_pos,
    logged_order,
    norm_gain,
    query_map,
    key_map,
    value_map,
    final_gain,
    score_vector,
):
    sections = lax.axis_size("section")
    replicas = lax.axis_size("dp")
    rows, width = prompts.shape
    chunks = rows // CHUNK
    kv_width = GROUPS * HEAD
    whole = pl.BlockSpec(memory_space=pltpu.VMEM)
    held = pl.BlockSpec(memory_space=pl.ANY)
    return pl.pallas_call(
        functools.partial(kernel, sections, replicas),
        out_shape=jax.ShapeDtypeStruct((replicas // sections,), F32),
        in_specs=[held] + [whole] * 7 + [held, held] + [whole] * 2,
        out_specs=pl.BlockSpec(memory_space=pltpu.SMEM),
        scratch_shapes=[
            pltpu.VMEM((rows, width), BF16),
            pltpu.VMEM((width, kv_width), BF16),
            pltpu.VMEM((width, kv_width), BF16),
            pltpu.VMEM((TAIL, 2 * kv_width), BF16),
            pltpu.VMEM((2 * HEAD, 2 * HEAD), BF16),
            pltpu.VMEM((GROUPS * WINDOW, kv_width), BF16),
            pltpu.VMEM((GROUPS * WINDOW, kv_width), BF16),
            pltpu.VMEM((chunks, CHUNK, GROUPS * WINDOW), F32),
            pltpu.VMEM((kv_width, GROUPS * WINDOW), BF16),
            pltpu.VMEM((GROUPS * WINDOW, kv_width), BF16),
            pltpu.VMEM((1, width), F32),
            pltpu.VMEM((8, 128), F32),
            pltpu.VMEM((8, 128), F32),
            pltpu.VMEM((8, 128), F32),
            pltpu.VMEM((replicas, 8, 128), F32),
            pltpu.VMEM((1, 128), F32),
            pltpu.SemaphoreType.DMA((chunks,)),
            pltpu.SemaphoreType.DMA((2, PIECES)),
            pltpu.SemaphoreType.DMA((chunks, PARTS)),
            pltpu.SemaphoreType.DMA((chunks, PARTS)),
            pltpu.SemaphoreType.DMA((1,)),
            pltpu.SemaphoreType.DMA((1,)),
            pltpu.SemaphoreType.DMA((sections,)),
            pltpu.SemaphoreType.DMA((1,)),
            pltpu.SemaphoreType.REGULAR,
        ],
        compiler_params=pltpu.CompilerParams(
            collective_id=0, has_side_effects=True, vmem_limit_bytes=56 << 20
        ),
        name="slates",
    )(
        prompts,
        dest_replica,
        anchor_start,
        pack_anchor,
        jnp.transpose(item_pos, (2, 0, 1)),
        jnp.transpose(logged_order, (2, 0, 1)),
        norm_gain,
        query_map,
        key_map,
        value_map,
        final_gain.reshape(1, width),
        score_vector,
    )


def solution(mesh):
    return jax.shard_map(
        body,
        mesh=mesh,
        in_specs=(
            P("dp", None),
            P("dp", None),
            P("dp", None),
            P("dp", None),
            P("dp", None),
            P("dp", None, None),
            P("dp", None, None),
            P("section", None),
            P("section", None, None),
            P("section", None, None),
            P("section", None, None),
            P(),
            P(),
        ),
        out_specs=P(("dp", "section")),
        check_vma=False,
    )
```

```python
import functools

import jax
import jax.numpy as jnp
from jax import lax
from jax.experimental import pallas as pl
from jax.experimental.pallas import tpu as pltpu
from jax.sharding import PartitionSpec as P

EPS = 1e-06
HEAD = 128
GROUPS = 4
ITEMS = 6
LMAX = 9
CHUNK = 16
TAIL = 16
WINDOW = CHUNK + TAIL
PARTS = 4

BF16 = jnp.bfloat16
F32 = jnp.float32
MESH = pl.DeviceIdType.MESH


def iota(shape, dim):
    return lax.broadcasted_iota(jnp.int32, shape, dim)


def kernel(
    sections,
    replicas,
    prompts,
    dest,
    start,
    pack,
    items,
    order,
    gain,
    query,
    key_map,
    value_map,
    final_gain,
    score_vector,
    out,
    x,
    kw,
    vw,
    kv,
    pair,
    kblock,
    vblock,
    bias,
    ones_q,
    ones_k,
    weigh,
    start_for,
    chosen,
    target,
    windows,
    leaving,
    gathered,
    final,
    w_sem,
    recv_sem,
    send_sem,
    score_send,
    score_recv,
    out_send,
    out_recv,
):
    d = lax.axis_index("dp")
    s = lax.axis_index("section")
    rows_all, width = x.shape
    chunks = rows_all // CHUNK
    last = sections - 1
    heads = width // HEAD
    per_group = heads // GROUPS
    kv_width = GROUPS * HEAD
    above = lax.rem(s + 1, sections)
    below = lax.rem(s + sections - 1, sections)

    def chunk_rows(c):
        return pl.ds(pl.multiple_of(c * CHUNK, 16), CHUNK)

    part = width // PARTS
    part_groups = GROUPS // PARTS

    def x_copy(c, p):
        cols = pl.ds(p * part, part)
        return pltpu.make_async_copy(
            prompts.at[chunk_rows(c), cols], x.at[chunk_rows(c), cols], recv_sem.at[c, p]
        )

    def hop(c, p):
        block = x.at[chunk_rows(c), pl.ds(p * part, part)]
        return pltpu.make_async_remote_copy(
            block, block, send_sem.at[c, p], recv_sem.at[c, p],
            device_id=(d, above), device_id_type=MESH,
        )

    def w_copies(p):
        rows = pl.ds(p * part, part)
        return [
            pltpu.make_async_copy(key_map.at[0, rows], kw.at[rows], w_sem.at[0, p]),
            pltpu.make_async_copy(value_map.at[0, rows], vw.at[rows], w_sem.at[1, p]),
        ]

    @pl.when(s == 0)
    def _():
        for p in range(PARTS):
            x_copy(0, p).start()

    for p in range(PARTS):
        for copy in w_copies(p):
            copy.start()

    @pl.when(s == 0)
    def _():
        def fetch(c, carry):
            for p in range(PARTS):
                x_copy(c, p).start()
            return carry

        lax.fori_loop(1, chunks, fetch, 0)

    barrier = pltpu.get_barrier_semaphore()
    pl.semaphore_signal(barrier, inc=1, device_id=(d, above), device_id_type=MESH)
    pl.semaphore_signal(barrier, inc=1, device_id=(d, below), device_id_type=MESH)

    @pl.when(s < last)
    def _():
        pl.semaphore_signal(barrier, inc=1, device_id=(d, last), device_id_type=MESH)

    @pl.when(s == last)
    def _():
        def greet_section(i, carry):
            pl.semaphore_signal(barrier, inc=1, device_id=(d, i), device_id_type=MESH)
            return carry

        def greet_replica(i, carry):
            peer = lax.rem(d + i, replicas)
            pl.semaphore_signal(barrier, inc=1, device_id=(peer, last), device_id_type=MESH)
            return carry

        lax.fori_loop(0, last, greet_section, 0)
        lax.fori_loop(1, replicas, greet_replica, 0)

    pair[...] = jnp.zeros_like(pair)
    pair[0:HEAD, 0:HEAD] = query[0]
    pair[HEAD : 2 * HEAD, HEAD : 2 * HEAD] = query[0]
    kblock[...] = jnp.zeros_like(kblock)
    vblock[...] = jnp.zeros_like(vblock)
    kv[0:TAIL, :] = jnp.zeros((TAIL, 2 * kv_width), BF16)
    ones_q[...] = jnp.where(
        iota(ones_q.shape, 0) // HEAD == iota(ones_q.shape, 1) // WINDOW, 1.0, 0.0
    ).astype(BF16)
    ones_k[...] = jnp.where(
        iota(ones_k.shape, 0) // WINDOW == iota(ones_k.shape, 1) // HEAD, 1.0, 0.0
    ).astype(BF16)

    starts = start[...].astype(F32)
    for c in range(chunks):
        row = (iota((CHUNK, replicas), 0) + c * CHUNK).astype(F32)
        first = jnp.max(jnp.where(starts <= row, starts, 0.0), axis=1, keepdims=True)
        seen = (iota((CHUNK, GROUPS * WINDOW), 1) % WINDOW + c * CHUNK - TAIL).astype(F32)
        own = (iota((CHUNK, GROUPS * WINDOW), 0) + c * CHUNK).astype(F32)
        bias[c] = jnp.where((seen >= first) & (seen <= own), 0.0, -1e30)

    square = (replicas, replicas)

    @pl.when(s == last)
    def _():
        weigh[...] = final_gain[...] * score_vector[...].astype(F32).reshape(1, width)
        diagonal = iota(square, 0) == iota(square, 1)

        def as_column(row):
            return jnp.sum(jnp.where(diagonal, row, 0.0), axis=1, keepdims=True)

        start_for[:, 0:1] = jnp.sum(
            jnp.where(dest[...] == iota(square, 0), starts, 0.0), axis=1, keepdims=True
        )
        away = pack[...] - d
        slot = jnp.where(away < 0, away + replicas, away).astype(F32)
        chosen[:, 0:replicas] = jnp.where(iota(square, 1).astype(F32) == as_column(slot), 1.0, 0.0)
        for k in range(ITEMS):
            spot = jnp.zeros((1, replicas), F32)
            for i in range(ITEMS):
                spot = spot + jnp.where(order[k] == i, items[i].astype(F32), 0.0)
            target[:, k : k + 1] = as_column(spot)
        windows[...] = jnp.zeros_like(windows)

    def meet():
        @pl.when(s < last)
        def _():
            pl.semaphore_wait(barrier, 3)

        @pl.when(s == last)
        def _():
            pl.semaphore_wait(barrier, last + replicas + 1)

    def scale_of(states):
        return lax.rsqrt(jnp.mean(states * states, axis=1, keepdims=True) + EPS)

    def by_group(parts):
        def head(b, j):
            a = (b % part_groups) * per_group + j
            p, half = divmod(a, 2)
            values = parts[b // part_groups]
            return values[p * CHUNK : (p + 1) * CHUNK, half * HEAD : (half + 1) * HEAD]

        return jnp.concatenate(
            [jnp.concatenate([head(b, j) for b in range(GROUPS)], axis=1) for j in range(per_group)],
            axis=0,
        )

    def block(c):
        rows = chunk_rows(c)
        old = kv[...]
        energy = jnp.zeros((CHUNK, 1), F32)
        keys = jnp.zeros((CHUNK, kv_width), F32)
        values = jnp.zeros((CHUNK, kv_width), F32)
        queries, squares = [], []
        for p in range(PARTS):
            hop(c, p).wait_recv()
            cols = slice(p * part, (p + 1) * part)
            states = x[rows, cols].astype(F32)
            energy = energy + jnp.sum(states * states, axis=1, keepdims=True)
            gained = (states * gain[:, cols]).astype(BF16)
            keys = keys + jnp.dot(gained, kw[cols, :], preferred_element_type=F32)
            values = values + jnp.dot(gained, vw[cols, :], preferred_element_type=F32)
            stacked = jnp.concatenate(
                [gained[:, i * 2 * HEAD : (i + 1) * 2 * HEAD] for i in range(part // (2 * HEAD))], axis=0
            )
            q = jnp.dot(stacked, pair[...], preferred_element_type=F32)
            queries.append(q.astype(BF16))
            squares.append((q * q).astype(BF16))
        scale = lax.rsqrt(energy * (1.0 / width) + EPS)
        keys = keys * scale
        values = (values * scale).astype(BF16)
        for b in range(GROUPS):
            cols = slice(b * HEAD, (b + 1) * HEAD)
            more = slice(kv_width + b * HEAD, kv_width + (b + 1) * HEAD)
            head = keys[:, cols]
            head = (head * scale_of(head)).astype(BF16)
            kblock[b * WINDOW : b * WINDOW + TAIL, cols] = old[:, cols]
            kblock[b * WINDOW + TAIL : (b + 1) * WINDOW, cols] = head
            kv[:, cols] = head
            vblock[b * WINDOW : b * WINDOW + TAIL, cols] = old[:, more]
            vblock[b * WINDOW + TAIL : (b + 1) * WINDOW, cols] = values[:, cols]
            kv[:, more] = values[:, cols]
        length = jnp.dot(by_group(squares), ones_q[...], preferred_element_type=F32)
        scales = jnp.concatenate([scale] * per_group, axis=0)
        factor = scales * lax.rsqrt(length * (scales * scales * (1.0 / HEAD)) + EPS) * HEAD ** (-0.5)
        raw = lax.dot_general(
            by_group(queries), kblock[...], (((1,), (1,)), ((), ())), preferred_element_type=F32
        )
        powers = jnp.exp(raw * factor + jnp.concatenate([bias[c]] * per_group, axis=0)).astype(BF16)
        for p in range(PARTS):
            near = slice(p * part_groups * HEAD, (p + 1) * part_groups * HEAD)
            cols = slice(p * part, (p + 1) * part)
            mixed = jnp.dot(powers, vblock[:, near], preferred_element_type=F32)
            total = jnp.dot(powers, ones_k[:, near], preferred_element_type=F32)
            mixed = mixed / total
            placed = [
                mixed[j * CHUNK : (j + 1) * CHUNK, b * HEAD : (b + 1) * HEAD]
                for b in range(part_groups)
                for j in range(per_group)
            ]
            x[rows, cols] = (x[rows, cols].astype(F32) + jnp.concatenate(placed, axis=1)).astype(BF16)

        @pl.when(c == 0)
        def _():
            meet()

        @pl.when(s < last)
        def _():
            for p in range(PARTS):
                hop(c, p).start()

    def finish(c):
        states = x[chunk_rows(c), :].astype(F32)
        value = jnp.sum(states * weigh[...], axis=1, keepdims=True) * scale_of(states)
        near = iota((CHUNK, CHUNK), 0) == iota((CHUNK, CHUNK), 1)
        scores = jnp.sum(jnp.where(near, value, 0.0), axis=0, keepdims=True)
        row = (iota((replicas, CHUNK), 1) + c * CHUNK).astype(F32)
        offset = row - start_for[:, 0:1]
        lane = iota(windows.shape, 1)
        fresh = jnp.zeros(windows.shape, F32)
        for i in range(LMAX):
            found = jnp.sum(jnp.where(offset == float(i), scores, 0.0), axis=1, keepdims=True)
            fresh = jnp.where(lane == i, found, fresh)
        windows[...] += fresh

    def advance(c, carry):
        block(c)

        @pl.when(s == last)
        def _():
            finish(c)

        return carry

    for p in range(PARTS):
        for copy in w_copies(p):
            copy.wait()

    lax.fori_loop(0, chunks, advance, 0)

    @pl.when(s == last)
    def _():
        def score_copy(i):
            peer = lax.rem(d + replicas - i, replicas)
            return pltpu.make_async_remote_copy(
                leaving.at[peer], gathered.at[i], score_send.at[0], score_recv.at[0],
                device_id=(peer, last), device_id_type=MESH,
            )

        leaving[:, 0, :] = windows[...]
        others = gathered.at[pl.ds(1, replicas - 1)]
        for i in range(1, replicas):
            score_copy(i).start()
        gathered[0] = leaving[d]
        pltpu.make_async_copy(others, others, score_recv.at[0]).wait()
        held = gathered[:, 0, :]
        taken = jnp.zeros(held.shape, F32)
        for i in range(replicas):
            taken = taken + chosen[:, i : i + 1] * held[i : i + 1, :]
        lane = iota(held.shape, 1).astype(F32)
        ordered = [
            jnp.sum(jnp.where(lane == target[:, k : k + 1], taken, 0.0), axis=1, keepdims=True)
            for k in range(ITEMS)
        ]
        tail = jnp.zeros((replicas, 1), F32)
        total = jnp.zeros((replicas, 1), F32)
        for k in reversed(range(ITEMS)):
            tail = tail + jnp.exp(ordered[k])
            total = total + (ordered[k] - jnp.log(tail))
        final[0:1, 0:replicas] = jnp.sum(
            jnp.where(iota(square, 0) == iota(square, 1), total, 0.0), axis=0, keepdims=True
        )

        def out_copy(i):
            return pltpu.make_async_remote_copy(
                final, final, out_send.at[i], out_recv.at[0], device_id=(d, i), device_id_type=MESH
            )

        for i in sorted(range(last), key=lambda i: -min(i + 1, last - i)):
            out_copy(i).start()
        pltpu.make_async_copy(others, others, score_send.at[0]).wait()
        for i in range(last):
            out_copy(i).wait_send()

    @pl.when(s < last)
    def _():
        def sent_hop(c, carry):
            for p in range(PARTS):
                hop(c, p).wait_send()
            return carry

        lax.fori_loop(0, chunks, sent_hop, 0)

    @pl.when(s < last)
    def _():
        pltpu.make_async_remote_copy(
            final, final, out_send.at[0], out_recv.at[0], device_id=(d, last), device_id_type=MESH
        ).wait_recv()

    values = final[...]
    share = replicas // sections
    for j in range(share):
        out[j] = jnp.sum(jnp.where(iota(values.shape, 1) == s * share + j, values, 0.0))


def body(
    prompts,
    dest_replica,
    anchor_start,
    pack_anchor,
    prompt_lengths,
    item_pos,
    logged_order,
    norm_gain,
    query_map,
    key_map,
    value_map,
    final_gain,
    score_vector,
):
    sections = lax.axis_size("section")
    replicas = lax.axis_size("dp")
    rows, width = prompts.shape
    chunks = rows // CHUNK
    kv_width = GROUPS * HEAD
    whole = pl.BlockSpec(memory_space=pltpu.VMEM)
    held = pl.BlockSpec(memory_space=pl.ANY)
    return pl.pallas_call(
        functools.partial(kernel, sections, replicas),
        out_shape=jax.ShapeDtypeStruct((replicas // sections,), F32),
        in_specs=[held] + [whole] * 7 + [held, held] + [whole] * 2,
        out_specs=pl.BlockSpec(memory_space=pltpu.SMEM),
        scratch_shapes=[
            pltpu.VMEM((rows, width), BF16),
            pltpu.VMEM((width, kv_width), BF16),
            pltpu.VMEM((width, kv_width), BF16),
            pltpu.VMEM((TAIL, 2 * kv_width), BF16),
            pltpu.VMEM((2 * HEAD, 2 * HEAD), BF16),
            pltpu.VMEM((GROUPS * WINDOW, kv_width), BF16),
            pltpu.VMEM((GROUPS * WINDOW, kv_width), BF16),
            pltpu.VMEM((chunks, CHUNK, GROUPS * WINDOW), F32),
            pltpu.VMEM((kv_width, GROUPS * WINDOW), BF16),
            pltpu.VMEM((GROUPS * WINDOW, kv_width), BF16),
            pltpu.VMEM((1, width), F32),
            pltpu.VMEM((replicas, 128), F32),
            pltpu.VMEM((replicas, 128), F32),
            pltpu.VMEM((replicas, 128), F32),
            pltpu.VMEM((replicas, 128), F32),
            pltpu.VMEM((replicas, 1, 128), F32),
            pltpu.VMEM((replicas, 1, 128), F32),
            pltpu.VMEM((1, 128), F32),
            pltpu.SemaphoreType.DMA((2, PARTS)),
            pltpu.SemaphoreType.DMA((chunks, PARTS)),
            pltpu.SemaphoreType.DMA((chunks, PARTS)),
            pltpu.SemaphoreType.DMA((1,)),
            pltpu.SemaphoreType.DMA((1,)),
            pltpu.SemaphoreType.DMA((sections,)),
            pltpu.SemaphoreType.DMA((1,)),
        ],
        compiler_params=pltpu.CompilerParams(
            collective_id=0, has_side_effects=True, vmem_limit_bytes=56 << 20
        ),
        name="slates",
    )(
        prompts,
        dest_replica,
        anchor_start,
        pack_anchor,
        jnp.transpose(item_pos, (2, 0, 1)),
        jnp.transpose(logged_order, (2, 0, 1)),
        norm_gain,
        query_map,
        key_map,
        value_map,
        final_gain.reshape(1, width),
        score_vector,
    )


def solution(mesh):
    return jax.shard_map(
        body,
        mesh=mesh,
        in_specs=(
            P("dp", None),
            P("dp", None),
            P("dp", None),
            P("dp", None),
            P("dp", None),
            P("dp", None, None),
            P("dp", None, None),
            P("section", None),
            P("section", None, None),
            P("section", None, None),
            P("section", None, None),
            P(),
            P(),
        ),
        out_specs=P(("dp", "section")),
        check_vma=False,
    )
```

```python
import functools

import jax
import jax.numpy as jnp
from jax import lax
from jax.experimental import pallas as pl
from jax.experimental.pallas import tpu as pltpu
from jax.sharding import PartitionSpec as P

EPS = 1e-06
HEAD = 128
GROUPS = 4
ITEMS = 6
LMAX = 9
CHUNK = 16
TAIL = 16
WINDOW = CHUNK + TAIL
PARTS = 4

BF16 = jnp.bfloat16
F32 = jnp.float32
MESH = pl.DeviceIdType.MESH


def iota(shape, dim):
    return lax.broadcasted_iota(jnp.int32, shape, dim)


def kernel(
    sections,
    replicas,
    prompts,
    dest_in,
    start_in,
    pack_in,
    items_in,
    order_in,
    gain_in,
    query_in,
    key_map,
    value_map,
    final_gain_in,
    score_vector_in,
    out,
    dest,
    start,
    pack,
    items,
    order,
    gain,
    query,
    final_gain,
    score_vector,
    in_sem,
    x,
    kw,
    vw,
    kv,
    pair,
    kblock,
    vblock,
    bias,
    ones_q,
    ones_k,
    weigh,
    start_for,
    chosen,
    target,
    windows,
    leaving,
    gathered,
    final,
    w_sem,
    recv_sem,
    send_sem,
    score_send,
    score_recv,
    out_send,
    out_recv,
):
    d = lax.axis_index("dp")
    s = lax.axis_index("section")
    rows_all, width = x.shape
    chunks = rows_all // CHUNK
    last = sections - 1
    heads = width // HEAD
    per_group = heads // GROUPS
    kv_width = GROUPS * HEAD
    above = lax.rem(s + 1, sections)
    below = lax.rem(s + sections - 1, sections)

    def chunk_rows(c):
        return pl.ds(pl.multiple_of(c * CHUNK, 16), CHUNK)

    part = width // PARTS
    part_pairs = heads // 2 // PARTS

    def x_copy(c, p):
        cols = pl.ds(p * part, part)
        return pltpu.make_async_copy(
            prompts.at[chunk_rows(c), cols], x.at[chunk_rows(c), cols], recv_sem.at[c, p]
        )

    def hop(c, p):
        block = x.at[chunk_rows(c), pl.ds(p * part, part)]
        return pltpu.make_async_remote_copy(
            block, block, send_sem.at[c, p], recv_sem.at[c, p],
            device_id=(d, above), device_id_type=MESH,
        )

    def w_copies(p):
        rows = pl.ds(p * part, part)
        return [
            pltpu.make_async_copy(key_map.at[0, rows], kw.at[rows], w_sem.at[0, p]),
            pltpu.make_async_copy(value_map.at[0, rows], vw.at[rows], w_sem.at[1, p]),
        ]

    @pl.when(s == 0)
    def _():
        for p in range(PARTS):
            x_copy(0, p).start()

    small = [
        pltpu.make_async_copy(source, held, in_sem.at[i])
        for i, (source, held) in enumerate(
            (
                (gain_in, gain),
                (query_in, query),
                (start_in, start),
                (dest_in, dest),
                (pack_in, pack),
                (items_in, items),
                (order_in, order),
                (final_gain_in, final_gain),
                (score_vector_in, score_vector),
            )
        )
    ]
    for copy in small[:3]:
        copy.start()
    for p in range(PARTS):
        for copy in w_copies(p):
            copy.start()
    for copy in small[3:]:
        copy.start()

    @pl.when(s == 0)
    def _():
        def fetch(c, carry):
            for p in range(PARTS):
                x_copy(c, p).start()
            return carry

        lax.fori_loop(1, chunks, fetch, 0)

    barrier = pltpu.get_barrier_semaphore()
    @pl.when(s > 0)
    def _():
        pl.semaphore_signal(barrier, inc=1, device_id=(d, below), device_id_type=MESH)

    @pl.when(s < last)
    def _():
        pl.semaphore_signal(barrier, inc=1, device_id=(d, last), device_id_type=MESH)

    @pl.when(s == last)
    def _():
        def greet_replica(i, carry):
            peer = lax.rem(d + i, replicas)
            pl.semaphore_signal(barrier, inc=1, device_id=(peer, last), device_id_type=MESH)
            return carry

        lax.fori_loop(1, replicas, greet_replica, 0)

    for copy in small[:3]:
        copy.wait()
    pair[...] = jnp.zeros_like(pair)
    pair[0:HEAD, 0:HEAD] = query[0]
    pair[HEAD : 2 * HEAD, HEAD : 2 * HEAD] = query[0]
    kblock[...] = jnp.zeros_like(kblock)
    vblock[...] = jnp.zeros_like(vblock)
    kv[0:TAIL, :] = jnp.zeros((TAIL, 2 * kv_width), BF16)
    ones_q[...] = jnp.where(
        iota(ones_q.shape, 0) // HEAD == iota(ones_q.shape, 1) // WINDOW, 1.0, 0.0
    ).astype(BF16)
    ones_k[...] = jnp.where(
        iota(ones_k.shape, 0) // WINDOW == iota(ones_k.shape, 1) // HEAD, 1.0, 0.0
    ).astype(BF16)

    starts = start[...].astype(F32)
    for c in range(chunks):
        row = (iota((CHUNK, replicas), 0) + c * CHUNK).astype(F32)
        first = jnp.max(jnp.where(starts <= row, starts, 0.0), axis=1, keepdims=True)
        seen = (iota((CHUNK, GROUPS * WINDOW), 1) % WINDOW + c * CHUNK - TAIL).astype(F32)
        own = (iota((CHUNK, GROUPS * WINDOW), 0) + c * CHUNK).astype(F32)
        bias[c] = jnp.where((seen >= first) & (seen <= own), 0.0, -1e30)

    square = (replicas, replicas)

    @pl.when(s == last)
    def _():
        for copy in small[3:]:
            copy.wait()
        weigh[...] = final_gain[...] * score_vector[...].astype(F32).reshape(1, width)
        diagonal = iota(square, 0) == iota(square, 1)

        def as_column(row):
            return jnp.sum(jnp.where(diagonal, row, 0.0), axis=1, keepdims=True)

        start_for[:, 0:1] = jnp.sum(
            jnp.where(dest[...] == iota(square, 0), starts, 0.0), axis=1, keepdims=True
        )
        away = pack[...] - d
        slot = jnp.where(away < 0, away + replicas, away).astype(F32)
        chosen[:, 0:replicas] = jnp.where(iota(square, 1).astype(F32) == as_column(slot), 1.0, 0.0)
        for k in range(ITEMS):
            spot = jnp.zeros((1, replicas), F32)
            for i in range(ITEMS):
                spot = spot + jnp.where(order[k] == i, items[i].astype(F32), 0.0)
            target[:, k : k + 1] = as_column(spot)
        windows[...] = jnp.zeros_like(windows)

    def meet():
        @pl.when(s < last)
        def _():
            pl.semaphore_wait(barrier, 1)

        @pl.when(s == last)
        def _():
            pl.semaphore_wait(barrier, last + replicas - 1)

    def scale_of(states):
        return lax.rsqrt(jnp.mean(states * states, axis=1, keepdims=True) + EPS)

    def by_group(parts):
        def head(b, j):
            pair_of, half = divmod(b * per_group + j, 2)
            home, p = divmod(pair_of, part_pairs)
            values = parts[home]
            return values[p * CHUNK : (p + 1) * CHUNK, half * HEAD : (half + 1) * HEAD]

        return jnp.concatenate(
            [jnp.concatenate([head(b, j) for b in range(GROUPS)], axis=1) for j in range(per_group)],
            axis=0,
        )

    def block(c):
        rows = chunk_rows(c)
        old = kv[...]
        energy = jnp.zeros((CHUNK, 1), F32)
        keys = jnp.zeros((CHUNK, kv_width), F32)
        values = jnp.zeros((CHUNK, kv_width), F32)
        queries, squares = [], []
        for p in range(PARTS):
            @pl.when(c == 0)
            def _():
                for copy in w_copies(p):
                    copy.wait()

            hop(c, p).wait_recv()
            cols = slice(p * part, (p + 1) * part)
            states = x[rows, cols].astype(F32)
            energy = energy + jnp.sum(states * states, axis=1, keepdims=True)
            gained = (states * gain[:, cols]).astype(BF16)
            keys = keys + jnp.dot(gained, kw[cols, :], preferred_element_type=F32)
            values = values + jnp.dot(gained, vw[cols, :], preferred_element_type=F32)
            stacked = jnp.concatenate(
                [gained[:, i * 2 * HEAD : (i + 1) * 2 * HEAD] for i in range(part // (2 * HEAD))], axis=0
            )
            q = jnp.dot(stacked, pair[...], preferred_element_type=F32)
            queries.append(q.astype(BF16))
            squares.append((q * q).astype(BF16))
        scale = lax.rsqrt(energy * (1.0 / width) + EPS)
        keys = keys * scale
        values = (values * scale).astype(BF16)
        for b in range(GROUPS):
            cols = slice(b * HEAD, (b + 1) * HEAD)
            more = slice(kv_width + b * HEAD, kv_width + (b + 1) * HEAD)
            head = keys[:, cols]
            head = (head * scale_of(head)).astype(BF16)
            kblock[b * WINDOW : b * WINDOW + TAIL, cols] = old[:, cols]
            kblock[b * WINDOW + TAIL : (b + 1) * WINDOW, cols] = head
            kv[:, cols] = head
            vblock[b * WINDOW : b * WINDOW + TAIL, cols] = old[:, more]
            vblock[b * WINDOW + TAIL : (b + 1) * WINDOW, cols] = values[:, cols]
            kv[:, more] = values[:, cols]
        length = jnp.dot(by_group(squares), ones_q[...], preferred_element_type=F32)
        scales = jnp.concatenate([scale] * per_group, axis=0)
        factor = scales * lax.rsqrt(length * (scales * scales * (1.0 / HEAD)) + EPS) * HEAD ** (-0.5)
        raw = lax.dot_general(
            by_group(queries), kblock[...], (((1,), (1,)), ((), ())), preferred_element_type=F32
        )
        powers = jnp.exp(raw * factor + jnp.concatenate([bias[c]] * per_group, axis=0)).astype(BF16)
        mixed = jnp.dot(powers, vblock[...], preferred_element_type=F32)
        mixed = mixed / jnp.dot(powers, ones_k[...], preferred_element_type=F32)
        placed = [
            mixed[j * CHUNK : (j + 1) * CHUNK, b * HEAD : (b + 1) * HEAD]
            for b in range(GROUPS)
            for j in range(per_group)
        ]
        x[rows, :] = (x[rows, :].astype(F32) + jnp.concatenate(placed, axis=1)).astype(BF16)

        @pl.when(c == 0)
        def _():
            meet()

        @pl.when(s < last)
        def _():
            for p in range(PARTS):
                hop(c, p).start()

    def finish(c):
        states = x[chunk_rows(c), :].astype(F32)
        value = jnp.sum(states * weigh[...], axis=1, keepdims=True) * scale_of(states)
        near = iota((CHUNK, CHUNK), 0) == iota((CHUNK, CHUNK), 1)
        scores = jnp.sum(jnp.where(near, value, 0.0), axis=0, keepdims=True)
        row = (iota((replicas, CHUNK), 1) + c * CHUNK).astype(F32)
        offset = row - start_for[:, 0:1]
        lane = iota(windows.shape, 1)
        fresh = jnp.zeros(windows.shape, F32)
        for i in range(LMAX):
            found = jnp.sum(jnp.where(offset == float(i), scores, 0.0), axis=1, keepdims=True)
            fresh = jnp.where(lane == i, found, fresh)
        windows[...] += fresh

    def advance(c, carry):
        block(c)

        @pl.when(s == last)
        def _():
            finish(c)

        return carry

    lax.fori_loop(0, chunks, advance, 0)

    @pl.when(s == last)
    def _():
        def score_copy(i):
            peer = lax.rem(d + replicas - i, replicas)
            return pltpu.make_async_remote_copy(
                leaving.at[peer], gathered.at[i], score_send.at[0], score_recv.at[0],
                device_id=(peer, last), device_id_type=MESH,
            )

        leaving[:, 0, :] = windows[...]
        others = gathered.at[pl.ds(1, replicas - 1)]
        for i in range(1, replicas):
            score_copy(i).start()
        gathered[0] = leaving[d]
        pltpu.make_async_copy(others, others, score_recv.at[0]).wait()
        held = gathered[:, 0, :]
        taken = jnp.zeros(held.shape, F32)
        for i in range(replicas):
            taken = taken + chosen[:, i : i + 1] * held[i : i + 1, :]
        lane = iota(held.shape, 1).astype(F32)
        ordered = [
            jnp.sum(jnp.where(lane == target[:, k : k + 1], taken, 0.0), axis=1, keepdims=True)
            for k in range(ITEMS)
        ]
        tail = jnp.zeros((replicas, 1), F32)
        total = jnp.zeros((replicas, 1), F32)
        for k in reversed(range(ITEMS)):
            tail = tail + jnp.exp(ordered[k])
            total = total + (ordered[k] - jnp.log(tail))
        final[0:1, 0:replicas] = jnp.sum(
            jnp.where(iota(square, 0) == iota(square, 1), total, 0.0), axis=0, keepdims=True
        )

        def out_copy(i):
            return pltpu.make_async_remote_copy(
                final, final, out_send.at[i], out_recv.at[0], device_id=(d, i), device_id_type=MESH
            )

        for i in sorted(range(last), key=lambda i: -min(i + 1, last - i)):
            out_copy(i).start()
        pltpu.make_async_copy(others, others, score_send.at[0]).wait()
        for i in range(last):
            out_copy(i).wait_send()

    @pl.when(s < last)
    def _():
        for copy in small[3:]:
            copy.wait()

        def sent_hop(c, carry):
            for p in range(PARTS):
                hop(c, p).wait_send()
            return carry

        lax.fori_loop(0, chunks, sent_hop, 0)

    @pl.when(s < last)
    def _():
        pltpu.make_async_remote_copy(
            final, final, out_send.at[0], out_recv.at[0], device_id=(d, last), device_id_type=MESH
        ).wait_recv()

    values = final[...]
    share = replicas // sections
    for j in range(share):
        out[j] = jnp.sum(jnp.where(iota(values.shape, 1) == s * share + j, values, 0.0))


def body(
    prompts,
    dest_replica,
    anchor_start,
    pack_anchor,
    prompt_lengths,
    item_pos,
    logged_order,
    norm_gain,
    query_map,
    key_map,
    value_map,
    final_gain,
    score_vector,
):
    sections = lax.axis_size("section")
    replicas = lax.axis_size("dp")
    rows, width = prompts.shape
    chunks = rows // CHUNK
    kv_width = GROUPS * HEAD
    held = pl.BlockSpec(memory_space=pl.ANY)
    return pl.pallas_call(
        functools.partial(kernel, sections, replicas),
        out_shape=jax.ShapeDtypeStruct((replicas // sections,), F32),
        in_specs=[held] * 12,
        out_specs=pl.BlockSpec(memory_space=pltpu.SMEM),
        scratch_shapes=[
            pltpu.VMEM((1, replicas), jnp.int32),
            pltpu.VMEM((1, replicas), jnp.int32),
            pltpu.VMEM((1, replicas), jnp.int32),
            pltpu.VMEM((ITEMS, 1, replicas), jnp.int32),
            pltpu.VMEM((ITEMS, 1, replicas), jnp.int32),
            pltpu.VMEM((1, width), F32),
            pltpu.VMEM((1, HEAD, HEAD), BF16),
            pltpu.VMEM((1, width), F32),
            pltpu.VMEM((width,), BF16),
            pltpu.SemaphoreType.DMA((9,)),
            pltpu.VMEM((rows, width), BF16),
            pltpu.VMEM((width, kv_width), BF16),
            pltpu.VMEM((width, kv_width), BF16),
            pltpu.VMEM((TAIL, 2 * kv_width), BF16),
            pltpu.VMEM((2 * HEAD, 2 * HEAD), BF16),
            pltpu.VMEM((GROUPS * WINDOW, kv_width), BF16),
            pltpu.VMEM((GROUPS * WINDOW, kv_width), BF16),
            pltpu.VMEM((chunks, CHUNK, GROUPS * WINDOW), F32),
            pltpu.VMEM((kv_width, GROUPS * WINDOW), BF16),
            pltpu.VMEM((GROUPS * WINDOW, kv_width), BF16),
            pltpu.VMEM((1, width), F32),
            pltpu.VMEM((replicas, 128), F32),
            pltpu.VMEM((replicas, 128), F32),
            pltpu.VMEM((replicas, 128), F32),
            pltpu.VMEM((replicas, 128), F32),
            pltpu.VMEM((replicas, 1, 128), F32),
            pltpu.VMEM((replicas, 1, 128), F32),
            pltpu.VMEM((1, 128), F32),
            pltpu.SemaphoreType.DMA((2, PARTS)),
            pltpu.SemaphoreType.DMA((chunks, PARTS)),
            pltpu.SemaphoreType.DMA((chunks, PARTS)),
            pltpu.SemaphoreType.DMA((1,)),
            pltpu.SemaphoreType.DMA((1,)),
            pltpu.SemaphoreType.DMA((sections,)),
            pltpu.SemaphoreType.DMA((1,)),
        ],
        compiler_params=pltpu.CompilerParams(
            collective_id=0, has_side_effects=True, vmem_limit_bytes=56 << 20
        ),
        name="slates",
    )(
        prompts,
        dest_replica,
        anchor_start,
        pack_anchor,
        jnp.transpose(item_pos, (2, 0, 1)),
        jnp.transpose(logged_order, (2, 0, 1)),
        norm_gain,
        query_map,
        key_map,
        value_map,
        final_gain.reshape(1, width),
        score_vector,
    )


def solution(mesh):
    return jax.shard_map(
        body,
        mesh=mesh,
        in_specs=(
            P("dp", None),
            P("dp", None),
            P("dp", None),
            P("dp", None),
            P("dp", None),
            P("dp", None, None),
            P("dp", None, None),
            P("section", None),
            P("section", None, None),
            P("section", None, None),
            P("section", None, None),
            P(),
            P(),
        ),
        out_specs=P(("dp", "section")),
        check_vma=False,
    )
```

```python
import functools

import jax
import jax.numpy as jnp
from jax import lax
from jax.experimental import pallas as pl
from jax.experimental.pallas import tpu as pltpu
from jax.sharding import PartitionSpec as P

EPS = 1e-06
HEAD = 128
GROUPS = 4
ITEMS = 6
LMAX = 9
CHUNK = 16
TAIL = 16
WINDOW = CHUNK + TAIL
PARTS = 5

BF16 = jnp.bfloat16
F32 = jnp.float32
MESH = pl.DeviceIdType.MESH


def iota(shape, dim):
    return lax.broadcasted_iota(jnp.int32, shape, dim)


def kernel(
    sections,
    replicas,
    prompts,
    dest_in,
    start_in,
    pack_in,
    items_in,
    order_in,
    gain_in,
    query_in,
    key_map,
    value_map,
    final_gain_in,
    score_vector_in,
    out,
    dest,
    start,
    pack,
    items,
    order,
    gain,
    query,
    final_gain,
    score_vector,
    in_sem,
    x,
    kw,
    vw,
    kv,
    pair,
    kblock,
    vblock,
    bias,
    ones_q,
    ones_k,
    weigh,
    start_for,
    chosen,
    target,
    windows,
    leaving,
    gathered,
    final,
    w_sem,
    recv_sem,
    send_sem,
    score_send,
    score_recv,
    out_send,
    out_recv,
):
    d = lax.axis_index("dp")
    s = lax.axis_index("section")
    rows_all, width = x.shape
    chunks = rows_all // CHUNK
    last = sections - 1
    heads = width // HEAD
    per_group = heads // GROUPS
    kv_width = GROUPS * HEAD
    above = lax.rem(s + 1, sections)
    below = lax.rem(s + sections - 1, sections)

    def chunk_rows(c):
        return pl.ds(pl.multiple_of(c * CHUNK, 16), CHUNK)

    part = width // PARTS
    part_pairs = heads // 2 // PARTS

    def x_copy(c, p):
        cols = pl.ds(p * part, part)
        return pltpu.make_async_copy(
            prompts.at[chunk_rows(c), cols], x.at[chunk_rows(c), cols], recv_sem.at[c, p]
        )

    def hop(c, p):
        block = x.at[chunk_rows(c), pl.ds(p * part, part)]
        return pltpu.make_async_remote_copy(
            block, block, send_sem.at[c, p], recv_sem.at[c, p],
            device_id=(d, above), device_id_type=MESH,
        )

    def w_copies(p):
        rows = pl.ds(p * part, part)
        return [
            pltpu.make_async_copy(key_map.at[0, rows], kw.at[rows], w_sem.at[0, p]),
            pltpu.make_async_copy(value_map.at[0, rows], vw.at[rows], w_sem.at[1, p]),
        ]

    @pl.when(s == 0)
    def _():
        for p in range(PARTS):
            x_copy(0, p).start()

    small = [
        pltpu.make_async_copy(source, held, in_sem.at[i])
        for i, (source, held) in enumerate(
            (
                (gain_in, gain),
                (query_in, query),
                (start_in, start),
                (dest_in, dest),
                (pack_in, pack),
                (items_in, items),
                (order_in, order),
                (final_gain_in, final_gain),
                (score_vector_in, score_vector),
            )
        )
    ]
    for copy in small[:3]:
        copy.start()
    for p in range(PARTS):
        for copy in w_copies(p):
            copy.start()
    for copy in small[3:]:
        copy.start()

    @pl.when(s == 0)
    def _():
        def fetch(c, carry):
            for p in range(PARTS):
                x_copy(c, p).start()
            return carry

        lax.fori_loop(1, chunks, fetch, 0)

    barrier = pltpu.get_barrier_semaphore()
    @pl.when(s > 0)
    def _():
        pl.semaphore_signal(barrier, inc=1, device_id=(d, below), device_id_type=MESH)

    @pl.when(s < last)
    def _():
        pl.semaphore_signal(barrier, inc=1, device_id=(d, last), device_id_type=MESH)

    @pl.when(s == last)
    def _():
        def greet_replica(i, carry):
            peer = lax.rem(d + i, replicas)
            pl.semaphore_signal(barrier, inc=1, device_id=(peer, last), device_id_type=MESH)
            return carry

        lax.fori_loop(1, replicas, greet_replica, 0)

    for copy in small[:3]:
        copy.wait()
    pair[...] = jnp.zeros_like(pair)
    pair[0:HEAD, 0:HEAD] = query[0]
    pair[HEAD : 2 * HEAD, HEAD : 2 * HEAD] = query[0]
    kblock[...] = jnp.zeros_like(kblock)
    vblock[...] = jnp.zeros_like(vblock)
    kv[0:TAIL, :] = jnp.zeros((TAIL, 2 * kv_width), BF16)
    ones_q[...] = jnp.where(
        iota(ones_q.shape, 0) // HEAD == iota(ones_q.shape, 1) // WINDOW, 1.0, 0.0
    ).astype(BF16)
    ones_k[...] = jnp.where(
        iota(ones_k.shape, 0) // WINDOW == iota(ones_k.shape, 1) // HEAD, 1.0, 0.0
    ).astype(BF16)

    starts = start[...].astype(F32)
    for c in range(chunks):
        row = (iota((CHUNK, replicas), 0) + c * CHUNK).astype(F32)
        first = jnp.max(jnp.where(starts <= row, starts, 0.0), axis=1, keepdims=True)
        seen = (iota((CHUNK, GROUPS * WINDOW), 1) % WINDOW + c * CHUNK - TAIL).astype(F32)
        own = (iota((CHUNK, GROUPS * WINDOW), 0) + c * CHUNK).astype(F32)
        bias[c] = jnp.where((seen >= first) & (seen <= own), 0.0, -1e30)

    square = (replicas, replicas)

    def steps_to(other):
        y = lax.rem(other // 8 - d // 8 + 4, 4)
        across = lax.rem(lax.rem(other // 2, 4) - lax.rem(d // 2, 4) + 4, 4)
        core = lax.rem(lax.rem(other, 2) - lax.rem(d, 2) + 2, 2)
        return y * 8 + across * 2 + core

    @pl.when(s == last)
    def _():
        for copy in small[3:]:
            copy.wait()
        weigh[...] = final_gain[...] * score_vector[...].astype(F32).reshape(1, width)
        diagonal = iota(square, 0) == iota(square, 1)

        def as_column(row):
            return jnp.sum(jnp.where(diagonal, row, 0.0), axis=1, keepdims=True)

        start_for[:, 0:1] = jnp.sum(
            jnp.where(dest[...] == iota(square, 0), starts, 0.0), axis=1, keepdims=True
        )
        slot = steps_to(pack[...]).astype(F32)
        chosen[:, 0:replicas] = jnp.where(iota(square, 1).astype(F32) == as_column(slot), 1.0, 0.0)
        for k in range(ITEMS):
            spot = jnp.zeros((1, replicas), F32)
            for i in range(ITEMS):
                spot = spot + jnp.where(order[k] == i, items[i].astype(F32), 0.0)
            target[:, k : k + 1] = as_column(spot)
        windows[...] = jnp.zeros_like(windows)

    def meet():
        @pl.when(s < last)
        def _():
            pl.semaphore_wait(barrier, 1)

        @pl.when(s == last)
        def _():
            pl.semaphore_wait(barrier, last + replicas - 1)

    def scale_of(states):
        return lax.rsqrt(jnp.mean(states * states, axis=1, keepdims=True) + EPS)

    def by_group(parts):
        def head(b, j):
            pair_of, half = divmod(b * per_group + j, 2)
            home, p = divmod(pair_of, part_pairs)
            values = parts[home]
            return values[p * CHUNK : (p + 1) * CHUNK, half * HEAD : (half + 1) * HEAD]

        return jnp.concatenate(
            [jnp.concatenate([head(b, j) for b in range(GROUPS)], axis=1) for j in range(per_group)],
            axis=0,
        )

    def block(c):
        rows = chunk_rows(c)
        old = kv[...]
        energy = jnp.zeros((CHUNK, 1), F32)
        keys = jnp.zeros((CHUNK, kv_width), F32)
        values = jnp.zeros((CHUNK, kv_width), F32)
        queries, squares = [], []
        for p in range(PARTS):
            @pl.when(c == 0)
            def _():
                for copy in w_copies(p):
                    copy.wait()

            hop(c, p).wait_recv()
            cols = slice(p * part, (p + 1) * part)
            states = x[rows, cols].astype(F32)
            energy = energy + jnp.sum(states * states, axis=1, keepdims=True)
            gained = (states * gain[:, cols]).astype(BF16)
            keys = keys + jnp.dot(gained, kw[cols, :], preferred_element_type=F32)
            values = values + jnp.dot(gained, vw[cols, :], preferred_element_type=F32)
            stacked = jnp.concatenate(
                [gained[:, i * 2 * HEAD : (i + 1) * 2 * HEAD] for i in range(part // (2 * HEAD))], axis=0
            )
            q = jnp.dot(stacked, pair[...], preferred_element_type=F32)
            queries.append(q.astype(BF16))
            squares.append((q * q).astype(BF16))
        scale = lax.rsqrt(energy * (1.0 / width) + EPS)
        keys = keys * scale
        values = (values * scale).astype(BF16)
        for b in range(GROUPS):
            cols = slice(b * HEAD, (b + 1) * HEAD)
            more = slice(kv_width + b * HEAD, kv_width + (b + 1) * HEAD)
            head = keys[:, cols]
            head = (head * scale_of(head)).astype(BF16)
            kblock[b * WINDOW : b * WINDOW + TAIL, cols] = old[:, cols]
            kblock[b * WINDOW + TAIL : (b + 1) * WINDOW, cols] = head
            kv[:, cols] = head
            vblock[b * WINDOW : b * WINDOW + TAIL, cols] = old[:, more]
            vblock[b * WINDOW + TAIL : (b + 1) * WINDOW, cols] = values[:, cols]
            kv[:, more] = values[:, cols]
        length = jnp.dot(by_group(squares), ones_q[...], preferred_element_type=F32)
        scales = jnp.concatenate([scale] * per_group, axis=0)
        factor = scales * lax.rsqrt(length * (scales * scales * (1.0 / HEAD)) + EPS) * HEAD ** (-0.5)
        raw = lax.dot_general(
            by_group(queries), kblock[...], (((1,), (1,)), ((), ())), preferred_element_type=F32
        )
        powers = jnp.exp(raw * factor + jnp.concatenate([bias[c]] * per_group, axis=0)).astype(BF16)
        mixed = jnp.dot(powers, vblock[...], preferred_element_type=F32)
        mixed = mixed / jnp.dot(powers, ones_k[...], preferred_element_type=F32)
        placed = [
            mixed[j * CHUNK : (j + 1) * CHUNK, b * HEAD : (b + 1) * HEAD]
            for b in range(GROUPS)
            for j in range(per_group)
        ]
        x[rows, :] = (x[rows, :].astype(F32) + jnp.concatenate(placed, axis=1)).astype(BF16)

        @pl.when(c == 0)
        def _():
            meet()

        @pl.when(s < last)
        def _():
            for p in range(PARTS):
                hop(c, p).start()

    def finish(c):
        states = x[chunk_rows(c), :].astype(F32)
        value = jnp.sum(states * weigh[...], axis=1, keepdims=True) * scale_of(states)
        near = iota((CHUNK, CHUNK), 0) == iota((CHUNK, CHUNK), 1)
        scores = jnp.sum(jnp.where(near, value, 0.0), axis=0, keepdims=True)
        row = (iota((replicas, CHUNK), 1) + c * CHUNK).astype(F32)
        offset = row - start_for[:, 0:1]
        lane = iota(windows.shape, 1)
        fresh = jnp.zeros(windows.shape, F32)
        for i in range(LMAX):
            found = jnp.sum(jnp.where(offset == float(i), scores, 0.0), axis=1, keepdims=True)
            fresh = jnp.where(lane == i, found, fresh)
        windows[...] += fresh

    def advance(c, carry):
        block(c)

        @pl.when(s == last)
        def _():
            finish(c)

        return carry

    lax.fori_loop(0, chunks, advance, 0)

    @pl.when(s == last)
    def _():
        def score_copy(i):
            y = lax.rem(d // 8 + 4 - i // 8, 4)
            across = lax.rem(lax.rem(d // 2, 4) + 4 - i // 2 % 4, 4)
            core = lax.rem(lax.rem(d, 2) + i, 2)
            peer = y * 8 + across * 2 + core
            return pltpu.make_async_remote_copy(
                leaving.at[peer], gathered.at[i], score_send.at[0], score_recv.at[0],
                device_id=(peer, last), device_id_type=MESH,
            )

        leaving[:, 0, :] = windows[...]
        others = gathered.at[pl.ds(1, replicas - 1)]
        def links(i):
            return min(i // 8, 4 - i // 8) + min(i // 2 % 4, 4 - i // 2 % 4)

        for i in sorted(range(1, replicas), key=lambda i: -links(i)):
            score_copy(i).start()
        gathered[0] = leaving[d]
        pltpu.make_async_copy(others, others, score_recv.at[0]).wait()
        held = gathered[:, 0, :]
        taken = jnp.zeros(held.shape, F32)
        for i in range(replicas):
            taken = taken + chosen[:, i : i + 1] * held[i : i + 1, :]
        lane = iota(held.shape, 1).astype(F32)
        ordered = [
            jnp.sum(jnp.where(lane == target[:, k : k + 1], taken, 0.0), axis=1, keepdims=True)
            for k in range(ITEMS)
        ]
        tail = jnp.zeros((replicas, 1), F32)
        total = jnp.zeros((replicas, 1), F32)
        for k in reversed(range(ITEMS)):
            tail = tail + jnp.exp(ordered[k])
            total = total + (ordered[k] - jnp.log(tail))
        final[0:1, 0:replicas] = jnp.sum(
            jnp.where(iota(square, 0) == iota(square, 1), total, 0.0), axis=0, keepdims=True
        )

        def out_copy(i):
            return pltpu.make_async_remote_copy(
                final, final, out_send.at[i], out_recv.at[0], device_id=(d, i), device_id_type=MESH
            )

        for i in sorted(range(last), key=lambda i: -min(i + 1, last - i)):
            out_copy(i).start()
        pltpu.make_async_copy(others, others, score_send.at[0]).wait()
        for i in range(last):
            out_copy(i).wait_send()

    @pl.when(s < last)
    def _():
        for copy in small[3:]:
            copy.wait()

        def sent_hop(c, carry):
            for p in range(PARTS):
                hop(c, p).wait_send()
            return carry

        lax.fori_loop(0, chunks, sent_hop, 0)

    @pl.when(s < last)
    def _():
        pltpu.make_async_remote_copy(
            final, final, out_send.at[0], out_recv.at[0], device_id=(d, last), device_id_type=MESH
        ).wait_recv()

    values = final[...]
    share = replicas // sections
    for j in range(share):
        out[j] = jnp.sum(jnp.where(iota(values.shape, 1) == s * share + j, values, 0.0))


def body(
    prompts,
    dest_replica,
    anchor_start,
    pack_anchor,
    prompt_lengths,
    item_pos,
    logged_order,
    norm_gain,
    query_map,
    key_map,
    value_map,
    final_gain,
    score_vector,
):
    sections = lax.axis_size("section")
    replicas = lax.axis_size("dp")
    rows, width = prompts.shape
    chunks = rows // CHUNK
    kv_width = GROUPS * HEAD
    held = pl.BlockSpec(memory_space=pl.ANY)
    return pl.pallas_call(
        functools.partial(kernel, sections, replicas),
        out_shape=jax.ShapeDtypeStruct((replicas // sections,), F32),
        in_specs=[held] * 12,
        out_specs=pl.BlockSpec(memory_space=pltpu.SMEM),
        scratch_shapes=[
            pltpu.VMEM((1, replicas), jnp.int32),
            pltpu.VMEM((1, replicas), jnp.int32),
            pltpu.VMEM((1, replicas), jnp.int32),
            pltpu.VMEM((ITEMS, 1, replicas), jnp.int32),
            pltpu.VMEM((ITEMS, 1, replicas), jnp.int32),
            pltpu.VMEM((1, width), F32),
            pltpu.VMEM((1, HEAD, HEAD), BF16),
            pltpu.VMEM((1, width), F32),
            pltpu.VMEM((width,), BF16),
            pltpu.SemaphoreType.DMA((9,)),
            pltpu.VMEM((rows, width), BF16),
            pltpu.VMEM((width, kv_width), BF16),
            pltpu.VMEM((width, kv_width), BF16),
            pltpu.VMEM((TAIL, 2 * kv_width), BF16),
            pltpu.VMEM((2 * HEAD, 2 * HEAD), BF16),
            pltpu.VMEM((GROUPS * WINDOW, kv_width), BF16),
            pltpu.VMEM((GROUPS * WINDOW, kv_width), BF16),
            pltpu.VMEM((chunks, CHUNK, GROUPS * WINDOW), F32),
            pltpu.VMEM((kv_width, GROUPS * WINDOW), BF16),
            pltpu.VMEM((GROUPS * WINDOW, kv_width), BF16),
            pltpu.VMEM((1, width), F32),
            pltpu.VMEM((replicas, 128), F32),
            pltpu.VMEM((replicas, 128), F32),
            pltpu.VMEM((replicas, 128), F32),
            pltpu.VMEM((replicas, 128), F32),
            pltpu.VMEM((replicas, 1, 128), F32),
            pltpu.VMEM((replicas, 1, 128), F32),
            pltpu.VMEM((1, 128), F32),
            pltpu.SemaphoreType.DMA((2, PARTS)),
            pltpu.SemaphoreType.DMA((chunks, PARTS)),
            pltpu.SemaphoreType.DMA((chunks, PARTS)),
            pltpu.SemaphoreType.DMA((1,)),
            pltpu.SemaphoreType.DMA((1,)),
            pltpu.SemaphoreType.DMA((sections,)),
            pltpu.SemaphoreType.DMA((1,)),
        ],
        compiler_params=pltpu.CompilerParams(
            collective_id=0, has_side_effects=True, vmem_limit_bytes=56 << 20
        ),
        name="slates",
    )(
        prompts,
        dest_replica,
        anchor_start,
        pack_anchor,
        jnp.transpose(item_pos, (2, 0, 1)),
        jnp.transpose(logged_order, (2, 0, 1)),
        norm_gain,
        query_map,
        key_map,
        value_map,
        final_gain.reshape(1, width),
        score_vector,
    )


def solution(mesh):
    return jax.shard_map(
        body,
        mesh=mesh,
        in_specs=(
            P("dp", None),
            P("dp", None),
            P("dp", None),
            P("dp", None),
            P("dp", None),
            P("dp", None, None),
            P("dp", None, None),
            P("section", None),
            P("section", None, None),
            P("section", None, None),
            P("section", None, None),
            P(),
            P(),
        ),
        out_specs=P(("dp", "section")),
        check_vma=False,
    )
```

```python
import functools

import jax
import jax.numpy as jnp
from jax import lax
from jax.experimental import pallas as pl
from jax.experimental.pallas import tpu as pltpu
from jax.sharding import PartitionSpec as P

EPS = 1e-06
HEAD = 128
GROUPS = 4
ITEMS = 6
LMAX = 9
CHUNK = 16
TAIL = 16
WINDOW = CHUNK + TAIL
PARTS = 4

BF16 = jnp.bfloat16
F32 = jnp.float32
MESH = pl.DeviceIdType.MESH


def iota(shape, dim):
    return lax.broadcasted_iota(jnp.int32, shape, dim)


def kernel(
    sections,
    replicas,
    prompts,
    dest_in,
    start_in,
    pack_in,
    items_in,
    order_in,
    gain_in,
    query_in,
    key_map,
    value_map,
    final_gain_in,
    score_vector_in,
    out,
    dest,
    start,
    pack,
    items,
    order,
    gain,
    query,
    final_gain,
    score_vector,
    in_sem,
    x,
    kw,
    vw,
    kv,
    pair,
    kblock,
    vblock,
    bias,
    ones_q,
    ones_k,
    weigh,
    start_for,
    chosen,
    target,
    windows,
    leaving,
    gathered,
    final,
    w_sem,
    recv_sem,
    send_sem,
    score_send,
    score_recv,
    out_send,
    out_recv,
):
    d = lax.axis_index("dp")
    s = lax.axis_index("section")
    rows_all, width = x.shape
    chunks = rows_all // CHUNK
    last = sections - 1
    heads = width // HEAD
    per_group = heads // GROUPS
    kv_width = GROUPS * HEAD
    above = lax.rem(s + 1, sections)
    below = lax.rem(s + sections - 1, sections)

    def chunk_rows(c):
        return pl.ds(pl.multiple_of(c * CHUNK, 16), CHUNK)

    part = width // PARTS
    part_pairs = heads // 2 // PARTS

    def x_copy(c, p):
        cols = pl.ds(p * part, part)
        return pltpu.make_async_copy(
            prompts.at[chunk_rows(c), cols], x.at[chunk_rows(c), cols], recv_sem.at[c, p]
        )

    def hop(c, p):
        block = x.at[chunk_rows(c), pl.ds(p * part, part)]
        return pltpu.make_async_remote_copy(
            block, block, send_sem.at[c, p], recv_sem.at[c, p],
            device_id=(d, above), device_id_type=MESH,
        )

    def w_copies(p):
        rows = pl.ds(p * part, part)
        return [
            pltpu.make_async_copy(key_map.at[0, rows], kw.at[rows], w_sem.at[0, p]),
            pltpu.make_async_copy(value_map.at[0, rows], vw.at[rows], w_sem.at[1, p]),
        ]

    @pl.when(s == 0)
    def _():
        for p in range(PARTS):
            x_copy(0, p).start()

    small = [
        pltpu.make_async_copy(source, held, in_sem.at[i])
        for i, (source, held) in enumerate(
            (
                (gain_in, gain),
                (query_in, query),
                (start_in, start),
                (dest_in, dest),
                (pack_in, pack),
                (items_in, items),
                (order_in, order),
                (final_gain_in, final_gain),
                (score_vector_in, score_vector),
            )
        )
    ]
    for copy in small[:3]:
        copy.start()
    for p in range(PARTS):
        for copy in w_copies(p):
            copy.start()
    for copy in small[3:]:
        copy.start()

    @pl.when(s == 0)
    def _():
        def fetch(c, carry):
            for p in range(PARTS):
                x_copy(c, p).start()
            return carry

        lax.fori_loop(1, chunks, fetch, 0)

    barrier = pltpu.get_barrier_semaphore()
    @pl.when(s > 0)
    def _():
        pl.semaphore_signal(barrier, inc=1, device_id=(d, below), device_id_type=MESH)

    @pl.when(s < last)
    def _():
        pl.semaphore_signal(barrier, inc=1, device_id=(d, last), device_id_type=MESH)

    @pl.when(s == last)
    def _():
        def greet_replica(i, carry):
            peer = lax.rem(d + i, replicas)
            pl.semaphore_signal(barrier, inc=1, device_id=(peer, last), device_id_type=MESH)
            return carry

        lax.fori_loop(1, replicas, greet_replica, 0)

    for copy in small[:3]:
        copy.wait()
    pair[...] = jnp.zeros_like(pair)
    pair[0:HEAD, 0:HEAD] = query[0]
    pair[HEAD : 2 * HEAD, HEAD : 2 * HEAD] = query[0]
    kblock[...] = jnp.zeros_like(kblock)
    vblock[...] = jnp.zeros_like(vblock)
    kv[0:TAIL, :] = jnp.zeros((TAIL, 2 * kv_width), BF16)
    ones_q[...] = jnp.where(
        iota(ones_q.shape, 0) // HEAD == iota(ones_q.shape, 1) // WINDOW, 1.0, 0.0
    ).astype(BF16)
    ones_k[...] = jnp.where(
        iota(ones_k.shape, 0) // WINDOW == iota(ones_k.shape, 1) // HEAD, 1.0, 0.0
    ).astype(BF16)

    starts = start[...].astype(F32)
    for c in range(chunks):
        row = (iota((CHUNK, replicas), 0) + c * CHUNK).astype(F32)
        first = jnp.max(jnp.where(starts <= row, starts, 0.0), axis=1, keepdims=True)
        seen = (iota((CHUNK, GROUPS * WINDOW), 1) % WINDOW + c * CHUNK - TAIL).astype(F32)
        own = (iota((CHUNK, GROUPS * WINDOW), 0) + c * CHUNK).astype(F32)
        bias[c] = jnp.where((seen >= first) & (seen <= own), 0.0, -1e30)

    square = (replicas, replicas)

    @pl.when(s == last)
    def _():
        for copy in small[3:]:
            copy.wait()
        weigh[...] = final_gain[...] * score_vector[...].astype(F32).reshape(1, width)
        diagonal = iota(square, 0) == iota(square, 1)

        def as_column(row):
            return jnp.sum(jnp.where(diagonal, row, 0.0), axis=1, keepdims=True)

        start_for[:, 0:1] = jnp.sum(
            jnp.where(dest[...] == iota(square, 0), starts, 0.0), axis=1, keepdims=True
        )
        away = pack[...] - d
        slot = jnp.where(away < 0, away + replicas, away).astype(F32)
        chosen[:, 0:replicas] = jnp.where(iota(square, 1).astype(F32) == as_column(slot), 1.0, 0.0)
        for k in range(ITEMS):
            spot = jnp.zeros((1, replicas), F32)
            for i in range(ITEMS):
                spot = spot + jnp.where(order[k] == i, items[i].astype(F32), 0.0)
            target[:, k : k + 1] = as_column(spot)
        windows[...] = jnp.zeros_like(windows)

    def meet():
        @pl.when(s < last)
        def _():
            pl.semaphore_wait(barrier, 1)

        @pl.when(s == last)
        def _():
            pl.semaphore_wait(barrier, last + replicas - 1)

    def scale_of(states):
        return lax.rsqrt(jnp.mean(states * states, axis=1, keepdims=True) + EPS)

    def by_group(parts):
        def head(b, j):
            pair_of, half = divmod(b * per_group + j, 2)
            home, p = divmod(pair_of, part_pairs)
            values = parts[home]
            return values[p * CHUNK : (p + 1) * CHUNK, half * HEAD : (half + 1) * HEAD]

        return jnp.concatenate(
            [jnp.concatenate([head(b, j) for b in range(GROUPS)], axis=1) for j in range(per_group)],
            axis=0,
        )

    def block(c, opening):
        rows = chunk_rows(c)
        old = kv[...]
        energy = jnp.zeros((CHUNK, 1), F32)
        keys = jnp.zeros((CHUNK, kv_width), F32)
        values = jnp.zeros((CHUNK, kv_width), F32)
        queries, squares = [], []
        for p in range(PARTS):
            if opening:
                for copy in w_copies(p):
                    copy.wait()

            hop(c, p).wait_recv()
            cols = slice(p * part, (p + 1) * part)
            states = x[rows, cols].astype(F32)
            energy = energy + jnp.sum(states * states, axis=1, keepdims=True)
            gained = (states * gain[:, cols]).astype(BF16)
            keys = keys + jnp.dot(gained, kw[cols, :], preferred_element_type=F32)
            values = values + jnp.dot(gained, vw[cols, :], preferred_element_type=F32)
            stacked = jnp.concatenate(
                [gained[:, i * 2 * HEAD : (i + 1) * 2 * HEAD] for i in range(part // (2 * HEAD))], axis=0
            )
            q = jnp.dot(stacked, pair[...], preferred_element_type=F32)
            queries.append(q.astype(BF16))
            squares.append((q * q).astype(BF16))
        scale = lax.rsqrt(energy * (1.0 / width) + EPS)
        keys = keys * scale
        values = (values * scale).astype(BF16)
        for b in range(GROUPS):
            cols = slice(b * HEAD, (b + 1) * HEAD)
            more = slice(kv_width + b * HEAD, kv_width + (b + 1) * HEAD)
            head = keys[:, cols]
            head = (head * scale_of(head)).astype(BF16)
            kblock[b * WINDOW : b * WINDOW + TAIL, cols] = old[:, cols]
            kblock[b * WINDOW + TAIL : (b + 1) * WINDOW, cols] = head
            kv[:, cols] = head
            vblock[b * WINDOW : b * WINDOW + TAIL, cols] = old[:, more]
            vblock[b * WINDOW + TAIL : (b + 1) * WINDOW, cols] = values[:, cols]
            kv[:, more] = values[:, cols]
        length = jnp.dot(by_group(squares), ones_q[...], preferred_element_type=F32)
        scales = jnp.concatenate([scale] * per_group, axis=0)
        factor = scales * lax.rsqrt(length * (scales * scales * (1.0 / HEAD)) + EPS) * HEAD ** (-0.5)
        raw = lax.dot_general(
            by_group(queries), kblock[...], (((1,), (1,)), ((), ())), preferred_element_type=F32
        )
        powers = jnp.exp(raw * factor + jnp.concatenate([bias[c]] * per_group, axis=0)).astype(BF16)
        mixed = jnp.dot(powers, vblock[...], preferred_element_type=F32)
        mixed = mixed / jnp.dot(powers, ones_k[...], preferred_element_type=F32)
        placed = [
            mixed[j * CHUNK : (j + 1) * CHUNK, b * HEAD : (b + 1) * HEAD]
            for b in range(GROUPS)
            for j in range(per_group)
        ]
        x[rows, :] = (x[rows, :].astype(F32) + jnp.concatenate(placed, axis=1)).astype(BF16)

        if opening:
            meet()

        @pl.when(s < last)
        def _():
            for p in range(PARTS):
                hop(c, p).start()

    def finish(c):
        states = x[chunk_rows(c), :].astype(F32)
        value = jnp.sum(states * weigh[...], axis=1, keepdims=True) * scale_of(states)
        near = iota((CHUNK, CHUNK), 0) == iota((CHUNK, CHUNK), 1)
        scores = jnp.sum(jnp.where(near, value, 0.0), axis=0, keepdims=True)
        row = (iota((replicas, CHUNK), 1) + c * CHUNK).astype(F32)
        offset = row - start_for[:, 0:1]
        lane = iota(windows.shape, 1)
        fresh = jnp.zeros(windows.shape, F32)
        for i in range(LMAX):
            found = jnp.sum(jnp.where(offset == float(i), scores, 0.0), axis=1, keepdims=True)
            fresh = jnp.where(lane == i, found, fresh)
        windows[...] += fresh

    def advance(c, carry):
        block(c, False)

        @pl.when(s == last)
        def _():
            finish(c)

        return carry

    block(0, True)

    @pl.when(s == last)
    def _():
        finish(0)

    lax.fori_loop(1, chunks, advance, 0)

    @pl.when(s == last)
    def _():
        def score_copy(i):
            peer = lax.rem(d + replicas - i, replicas)
            return pltpu.make_async_remote_copy(
                leaving.at[peer], gathered.at[i], score_send.at[0], score_recv.at[0],
                device_id=(peer, last), device_id_type=MESH,
            )

        leaving[:, 0, :] = windows[...]
        others = gathered.at[pl.ds(1, replicas - 1)]
        for i in range(1, replicas):
            score_copy(i).start()
        gathered[0] = leaving[d]
        pltpu.make_async_copy(others, others, score_recv.at[0]).wait()
        held = gathered[:, 0, :]
        taken = jnp.zeros(held.shape, F32)
        for i in range(replicas):
            taken = taken + chosen[:, i : i + 1] * held[i : i + 1, :]
        lane = iota(held.shape, 1).astype(F32)
        ordered = [
            jnp.sum(jnp.where(lane == target[:, k : k + 1], taken, 0.0), axis=1, keepdims=True)
            for k in range(ITEMS)
        ]
        tail = jnp.zeros((replicas, 1), F32)
        total = jnp.zeros((replicas, 1), F32)
        for k in reversed(range(ITEMS)):
            tail = tail + jnp.exp(ordered[k])
            total = total + (ordered[k] - jnp.log(tail))
        final[0:1, 0:replicas] = jnp.sum(
            jnp.where(iota(square, 0) == iota(square, 1), total, 0.0), axis=0, keepdims=True
        )

        def out_copy(i):
            return pltpu.make_async_remote_copy(
                final, final, out_send.at[i], out_recv.at[0], device_id=(d, i), device_id_type=MESH
            )

        for i in sorted(range(last), key=lambda i: -min(i + 1, last - i)):
            out_copy(i).start()
        pltpu.make_async_copy(others, others, score_send.at[0]).wait()
        for i in range(last):
            out_copy(i).wait_send()

    @pl.when(s < last)
    def _():
        for copy in small[3:]:
            copy.wait()

        def sent_hop(c, carry):
            for p in range(PARTS):
                hop(c, p).wait_send()
            return carry

        lax.fori_loop(0, chunks, sent_hop, 0)

    @pl.when(s < last)
    def _():
        pltpu.make_async_remote_copy(
            final, final, out_send.at[0], out_recv.at[0], device_id=(d, last), device_id_type=MESH
        ).wait_recv()

    values = final[...]
    share = replicas // sections
    for j in range(share):
        out[j] = jnp.sum(jnp.where(iota(values.shape, 1) == s * share + j, values, 0.0))


def body(
    prompts,
    dest_replica,
    anchor_start,
    pack_anchor,
    prompt_lengths,
    item_pos,
    logged_order,
    norm_gain,
    query_map,
    key_map,
    value_map,
    final_gain,
    score_vector,
):
    sections = lax.axis_size("section")
    replicas = lax.axis_size("dp")
    rows, width = prompts.shape
    chunks = rows // CHUNK
    kv_width = GROUPS * HEAD
    held = pl.BlockSpec(memory_space=pl.ANY)
    return pl.pallas_call(
        functools.partial(kernel, sections, replicas),
        out_shape=jax.ShapeDtypeStruct((replicas // sections,), F32),
        in_specs=[held] * 12,
        out_specs=pl.BlockSpec(memory_space=pltpu.SMEM),
        scratch_shapes=[
            pltpu.VMEM((1, replicas), jnp.int32),
            pltpu.VMEM((1, replicas), jnp.int32),
            pltpu.VMEM((1, replicas), jnp.int32),
            pltpu.VMEM((ITEMS, 1, replicas), jnp.int32),
            pltpu.VMEM((ITEMS, 1, replicas), jnp.int32),
            pltpu.VMEM((1, width), F32),
            pltpu.VMEM((1, HEAD, HEAD), BF16),
            pltpu.VMEM((1, width), F32),
            pltpu.VMEM((width,), BF16),
            pltpu.SemaphoreType.DMA((9,)),
            pltpu.VMEM((rows, width), BF16),
            pltpu.VMEM((width, kv_width), BF16),
            pltpu.VMEM((width, kv_width), BF16),
            pltpu.VMEM((TAIL, 2 * kv_width), BF16),
            pltpu.VMEM((2 * HEAD, 2 * HEAD), BF16),
            pltpu.VMEM((GROUPS * WINDOW, kv_width), BF16),
            pltpu.VMEM((GROUPS * WINDOW, kv_width), BF16),
            pltpu.VMEM((chunks, CHUNK, GROUPS * WINDOW), F32),
            pltpu.VMEM((kv_width, GROUPS * WINDOW), BF16),
            pltpu.VMEM((GROUPS * WINDOW, kv_width), BF16),
            pltpu.VMEM((1, width), F32),
            pltpu.VMEM((replicas, 128), F32),
            pltpu.VMEM((replicas, 128), F32),
            pltpu.VMEM((replicas, 128), F32),
            pltpu.VMEM((replicas, 128), F32),
            pltpu.VMEM((replicas, 1, 128), F32),
            pltpu.VMEM((replicas, 1, 128), F32),
            pltpu.VMEM((1, 128), F32),
            pltpu.SemaphoreType.DMA((2, PARTS)),
            pltpu.SemaphoreType.DMA((chunks, PARTS)),
            pltpu.SemaphoreType.DMA((chunks, PARTS)),
            pltpu.SemaphoreType.DMA((1,)),
            pltpu.SemaphoreType.DMA((1,)),
            pltpu.SemaphoreType.DMA((sections,)),
            pltpu.SemaphoreType.DMA((1,)),
        ],
        compiler_params=pltpu.CompilerParams(
            collective_id=0, has_side_effects=True, vmem_limit_bytes=56 << 20
        ),
        name="slates",
    )(
        prompts,
        dest_replica,
        anchor_start,
        pack_anchor,
        jnp.transpose(item_pos, (2, 0, 1)),
        jnp.transpose(logged_order, (2, 0, 1)),
        norm_gain,
        query_map,
        key_map,
        value_map,
        final_gain.reshape(1, width),
        score_vector,
    )


def solution(mesh):
    return jax.shard_map(
        body,
        mesh=mesh,
        in_specs=(
            P("dp", None),
            P("dp", None),
            P("dp", None),
            P("dp", None),
            P("dp", None),
            P("dp", None, None),
            P("dp", None, None),
            P("section", None),
            P("section", None, None),
            P("section", None, None),
            P("section", None, None),
            P(),
            P(),
        ),
        out_specs=P(("dp", "section")),
        check_vma=False,
    )
```
